32 devices in a mesh: groups: 2 (over y), expert: 4 (over x, core), tensor: 4 (over z).
Axes of the slice: x: 2, y: 2, z: 4, core: 2. Of those that a mesh axis runs over, the one named last changes fastest.
Arguments:
- residual: bfloat16 [512, 7168], P(('groups', 'expert'), 'tensor'), parts along dimension 0
- attn_partial: bfloat16 [4, 512, 7168], P('tensor', ('groups', 'expert')), parts along dimension 1, may hold values from -4 to 4
- norm_gain: bfloat16 [7168], P('tensor'), may hold values from 0.25 to 1.75
- expert_ids: int32 [512, 2], P(('groups', 'expert')), parts along dimension 0, may hold values from 0 to 3, all different within a row; in each aligned block of 64 rows (0 to 63, 64 to 127, ...) at most 40 rows name the same one
- route_scores: float32 [512, 2], P(('groups', 'expert')), parts along dimension 0, may hold values from 0.05 to 1
- w_gate: bfloat16 [4, 7168, 2048], P('expert', 'tensor'), may hold values from -0.0625 to 0.0625
- w_down: bfloat16 [4, 2048, 7168], P('expert', None, 'tensor'), may hold values from -0.125 to 0.125
Outputs:
- stream: bfloat16 [512, 7168], P(('groups', 'expert'), 'tensor'), parts along dimension 0
- moe_out: bfloat16 [512, 7168], P(('groups', 'expert'), 'tensor'), parts along dimension 0
The draws below stay inside these ranges and needn't reach their ends.
There are 2 independent parts, one for each index of `groups`. The reference program is written for one: setup_inputs(seed, part) draws one part's arguments, and reference() takes and returns one part's arrays. A program takes and returns all parts, laid end to end along the dimension named above; an argument that names none is the same for every part. Nothing has to cross between parts.
Inputs may be any that keep to these rules, and one draw needn't show every extreme that they name: `expert_ids`: in each device's block of 64 tokens no expert is named by more than 40 rows, a bound that some block reaches; a token names 2 different experts.
All inputs are finite; a program needn't handle non-finite values.
Results may differ from the reference program's by a relative error of at most 0.018.
Values may be sent and summed in bfloat16 or wider, within the bound.
No kernel may reach another device: no remote copies, remote signals or barrier semaphores. Data moves between devices by JAX's collectives and lax.ppermute only.
A program may use at most 64 MiB of HBM per device.

```python
import math
import jax
import jax.numpy as jnp
import numpy as np
from jax import lax

D = 7168
FF = 2048
TOK_DEV = 64
TPARTS = 4
EXPERTS = 4
TOP = 2
CAP = 40
TOKENS = 256


def draw_residual(key, part):
    key = jax.random.fold_in(key, 11)
    first, second, third = jax.random.split(key, 3)
    columns = jnp.arange(D).astype(jnp.float32)
    col_scale = jnp.exp(math.log(3.0) * columns / D + jax.random.uniform(second, (D,), jnp.float32, 0.0, math.log(3.3)))
    base = jax.random.normal(first, (TOKENS, D), jnp.float32)
    row_scale = jnp.exp(jax.random.uniform(third, (TOKENS, 1), jnp.float32, 0.0, math.log(10.0)))
    return (0.3 * base * row_scale * col_scale[None, :]).astype(jnp.bfloat16)


def steps_of(own_key, extent, pieces, smallest, largest):
    level, own = 1.0, jax.random.fold_in(own_key, 6)
    for axis_at, parts in pieces:
        steps = jnp.exp(jax.random.uniform(jax.random.fold_in(own, axis_at), (parts,), jnp.float32, smallest / len(pieces), largest / len(pieces)))
        level = level * jnp.repeat(steps, extent[axis_at] // parts).reshape([-1 if axis == axis_at else 1 for axis in range(len(extent))])
    return level


def assign_block(rng, own, number, rows, count, top, most, slope):
    ranking = jax.random.permutation(rng, count)
    packed, common = portions_of(count, rows * top, most, slope, True), portions_of(count, rows * top, most, slope, False)
    places = jnp.arange(count)

    def named(tallies, rotation):
        used = int((tallies > 0).sum())
        fixed = max(1, used // 4)
        moved = fixed + (places - fixed + rotation * (used - fixed)) % max(1, count - fixed)
        return jnp.zeros((count,), jnp.int32).at[ranking[jnp.where(places < fixed, places, moved)]].set(jnp.asarray(tallies, jnp.int32))

    tallies = jnp.where(number % 4 == 0, named(packed, number // 4), named(common, number - number // 4 - 1))
    mixed = jax.random.permutation(jax.random.fold_in(own, 3), count)
    source_of, receiver = mixed[0:count // 2 * 2:2], mixed[1:count // 2 * 2:2]
    room = jnp.minimum(tallies[source_of] - 1, most - tallies[receiver]) // 2
    room = jnp.where((source_of == ranking[0]) | (receiver == ranking[0]) | (tallies[receiver] == 0), 0, jnp.maximum(room, 0))
    moved = jax.random.randint(jax.random.fold_in(own, 4), (count // 2,), 0, 1 << 20) % (room + 1)
    tallies = tallies.at[source_of].add(-moved).at[receiver].add(moved)
    labels = jnp.searchsorted(jnp.cumsum(tallies), jnp.arange(rows * top), side="right").astype(jnp.int32)
    listing = labels.reshape(top, rows).T
    listing = listing[jax.random.permutation(jax.random.fold_in(own, 1), rows)]
    rotation = jax.random.randint(jax.random.fold_in(own, 2), (rows, 1), 0, top)
    return jnp.take_along_axis(listing, (jnp.arange(top)[None, :] + rotation) % top, axis=1)


def portions_of(count, total, limit, skew, full):
    loads = [(1 << 20) // math.isqrt(standing ** skew) + 1 for standing in range(1, count + 1)]
    largest = limit if full else min(limit, max(-(-total // count), total * loads[0] // sum(loads)))
    least = 1 if total - largest >= count - 1 else 0
    counts, rest = [largest] + [least] * (count - 1), total - largest - least * (count - 1)
    while rest > 0:
        movable = [i for i in range(1, count) if counts[i] < largest] or [i for i in range(1, count) if counts[i] < limit]
        whole, left = sum([loads[i] for i in movable]), rest
        for i in movable:
            extra = min(limit - counts[i], max(1, left * loads[i] // whole), rest)
            counts[i] = counts[i] + extra
            rest = rest - extra
    return np.array(counts)


def noise(key, extent, width, limit, pieces=(), held_as=jnp.bfloat16):
    factor_of = steps_of(key, extent, pieces, -0.22, 0.18) if pieces else 1.0
    array = jax.random.normal(key, extent, jnp.float32) * width * factor_of
    return jnp.minimum(jnp.maximum(array, -limit), limit).astype(held_as)


def setup_inputs(seed: int = 0, part: int = 0) -> dict:
    key_list = jax.random.split(jax.random.key(seed), 8)
    part_splits = jax.random.split(jax.random.fold_in(key_list[7], part), 8)
    residual = draw_residual(jax.random.fold_in(jax.random.fold_in(key_list[7], part), 71), part)
    attn_partial = noise(part_splits[1], (TPARTS, TOKENS, D), 0.5, 4.0, ((0, 4), (1, 4)))
    norm_gain = jnp.clip(1.0 + 0.15 * jax.random.normal(key_list[2], (D,), jnp.float32), 0.25, 1.75).astype(jnp.bfloat16)
    expert_ids_keys = jax.random.split(jax.random.fold_in(part_splits[3], 1), TOKENS // TOK_DEV)
    expert_ids_turns = jax.random.permutation(jax.random.fold_in(part_splits[3], 3), TOKENS // TOK_DEV)
    expert_ids = jax.vmap(lambda own, number: assign_block(jax.random.fold_in(part_splits[3], 2), own, number, TOK_DEV, EXPERTS, TOP, CAP, 2))(expert_ids_keys, expert_ids_turns).reshape((TOKENS, TOP))
    route_scores = jnp.clip(jnp.exp(math.log(1.0) - 2.9957323 * jax.random.uniform(part_splits[4], (TOKENS, TOP), jnp.float32) ** steps_of(part_splits[4], (TOKENS, TOP), ((0, 4),), -0.2, 0.2)), 0.05, 1.0)
    w_gate = noise(key_list[5], (EXPERTS, D, FF), D ** -0.5, 0.0625, ((0, 4), (1, 4)))
    w_down = noise(key_list[6], (EXPERTS, FF, D), FF ** -0.5, 0.125, ((0, 4), (2, 4)))
    return dict(residual=residual, attn_partial=attn_partial, norm_gain=norm_gain, expert_ids=expert_ids, route_scores=route_scores, w_gate=w_gate, w_down=w_down)


def reference(residual, attn_partial, norm_gain, expert_ids, route_scores, w_gate, w_down):
    whole = residual.astype(jnp.float32) + lax.optimization_barrier(jnp.sum(attn_partial.astype(jnp.float32), axis=0))
    stream = whole.astype(jnp.bfloat16)
    inverse = lax.rsqrt(lax.optimization_barrier(jnp.mean(whole * whole, axis=1)) + 1e-06)
    normed = (whole * inverse[:, None] * norm_gain.astype(jnp.float32)).astype(jnp.bfloat16)
    weights = 2.827 * route_scores / lax.optimization_barrier(jnp.sum(route_scores, axis=1, keepdims=True))
    width_share = D // TPARTS
    blocked = normed.astype(jnp.float32).reshape(TOKENS, TPARTS, width_share)

    def one_expert(total, index):
        gate_block = w_gate[index].astype(jnp.float32).reshape(TPARTS, width_share, FF)
        partial_value = jnp.einsum('tnd,ndf->tnf', blocked, gate_block)
        gate = lax.optimization_barrier(jnp.sum(partial_value.astype(jnp.bfloat16).astype(jnp.float32), axis=1))
        hidden = jax.nn.silu(gate).astype(jnp.bfloat16)
        result = jnp.dot(hidden, w_down[index], preferred_element_type=jnp.float32).astype(jnp.bfloat16)
        coef = lax.optimization_barrier(jnp.sum(jnp.where(expert_ids == index, weights, 0.0), axis=1))
        return (total + coef[:, None] * result.astype(jnp.float32), None)
    start = jnp.zeros((TOKENS, D), jnp.float32)
    total, unused = lax.scan(one_expert, start, jnp.arange(EXPERTS, dtype=jnp.int32))
    return (stream, total.astype(jnp.bfloat16))
```

```python
import functools

import jax
import jax.numpy as jnp
from jax import lax
from jax.experimental import pallas as pl
from jax.experimental.pallas import tpu as pltpu
from jax.sharding import PartitionSpec as P

EXTRA = 8


def partners(n):
    return list(range(n - 1, -1, -1))


def exchange(value, axis, step):
    n = lax.axis_size(axis)
    return lax.ppermute(value, axis, [(i, i ^ step) for i in range(n)])


def params(mib=24):
    return pltpu.CompilerParams(vmem_limit_bytes=mib << 20)


def whole():
    return pl.BlockSpec(memory_space=pltpu.VMEM)


def scalar():
    return pl.BlockSpec(memory_space=pltpu.SMEM)


def routing_kernel(n, cap, me_ref, ids_ref, idst_ref, scores_ref, select_ref, high_ref, low_ref):
    me = me_ref[0]
    tokens, top = ids_ref.shape
    f32, bf16 = jnp.float32, jnp.bfloat16
    row = lax.broadcasted_iota(jnp.int32, (tokens, tokens), 0)
    col = lax.broadcasted_iota(jnp.int32, (tokens, tokens), 1)
    before_t = jnp.where(row < col, 1.0, 0.0).astype(bf16)
    before = jnp.where(col < row, 1.0, 0.0).astype(bf16)
    scores = scores_ref[...]
    weights = 2.827 * scores / jnp.sum(scores, axis=1, keepdims=True)
    slot_t = lax.broadcasted_iota(jnp.int32, (cap, tokens), 0)
    slot = lax.broadcasted_iota(jnp.int32, (tokens, cap), 1)
    selects, highs, lows = [], [], []
    for k in range(n):
        expert = me ^ k
        named_t = jnp.zeros((1, tokens), f32)
        named = jnp.zeros((tokens, 1), f32)
        weight = jnp.zeros((tokens, 1), f32)
        for j in range(top):
            hit = jnp.where(ids_ref[:, j : j + 1] == expert, 1.0, 0.0)
            named_t += jnp.where(idst_ref[j : j + 1, :] == expert, 1.0, 0.0)
            named += hit
            weight += hit * weights[:, j : j + 1]
        place_t = jnp.dot(
            jnp.broadcast_to(named_t, (8, tokens)).astype(bf16), before_t, preferred_element_type=f32
        )[0:1, :].astype(jnp.int32)
        place = jnp.dot(
            before, jnp.broadcast_to(named, (tokens, 128)).astype(bf16), preferred_element_type=f32
        )[:, 0:1].astype(jnp.int32)
        selects.append(jnp.where(place_t == slot_t, jnp.broadcast_to(named_t, slot_t.shape), 0.0))
        full = jnp.where(place == slot, jnp.broadcast_to(weight, slot.shape), 0.0)
        high = full.astype(bf16).astype(f32)
        highs.append(high)
        lows.append(full - high)
    select_ref[...] = jnp.concatenate(selects, axis=0).astype(bf16)
    high_ref[...] = jnp.concatenate(highs, axis=1).astype(bf16)
    low_ref[...] = jnp.concatenate(lows, axis=1).astype(bf16)


def pack_kernel(n_tensor, n, cap, residual_ref, select_ref, *refs):
    parts, stream_ref, outs = refs[:n_tensor], refs[n_tensor], refs[n_tensor + 1 :]
    total = residual_ref[...].astype(jnp.float32)
    for part in parts:
        total += part[...].astype(jnp.float32)
    stream = total.astype(jnp.bfloat16)
    stream_ref[...] = stream
    packed = jnp.dot(select_ref[...], stream, preferred_element_type=jnp.float32)
    for k in range(n):
        outs[k][...] = packed[k * cap : (k + 1) * cap, :].astype(jnp.bfloat16)


def prepare_kernel(n, gain_ref, *refs):
    pieces, lhs_ref, squares_ref = refs[:n], refs[n], refs[n + 1]
    rows = jnp.concatenate([p[...].astype(jnp.float32) for p in pieces], axis=0)
    squared = (rows * rows).astype(jnp.bfloat16)
    ones = jnp.ones((8, rows.shape[1]), jnp.bfloat16)
    sums = lax.dot_general(ones, squared, (((1,), (1,)), ((), ())), preferred_element_type=jnp.float32)
    high = sums.astype(jnp.bfloat16).astype(jnp.float32)
    low = sums - high
    which = lax.broadcasted_iota(jnp.int32, sums.shape, 0)
    squares_ref[...] = jnp.where(which == 0, high, jnp.where(which == 1, low, 0.0))
    lhs_ref[...] = (rows * gain_ref[...].astype(jnp.float32)).astype(jnp.bfloat16)


def gate_kernel(block_ref, lhs_ref, squares_ref, w_ref, out_ref):
    rows = lhs_ref.shape[0]
    width = out_ref.shape[1]
    product = jnp.dot(lhs_ref[...], w_ref[0], preferred_element_type=jnp.float32)
    squares = squares_ref[...]
    if rows <= width:
        extra = jnp.concatenate([squares, jnp.zeros((EXTRA, width - rows), jnp.float32)], axis=1)
    else:
        extra = jnp.concatenate(
            [squares[0:2, i : i + width] for i in range(0, rows, width)]
            + [jnp.zeros((extra_rows(rows, width) - 2 * (rows // width), width), jnp.float32)],
            axis=0,
        )
    out_ref[...] = jnp.concatenate([product, extra], axis=0).astype(jnp.bfloat16)


def extra_rows(rows, width):
    return EXTRA if rows <= width else -(-2 * (rows // width) // 8) * 8


def activate_kernel(n, rows, features, *refs):
    parts, out_ref = refs[:n], refs[n]
    f32, bf16 = jnp.float32, jnp.bfloat16
    width = out_ref.shape[1]
    total, squares = None, None
    for part in parts:
        value = part[...].astype(f32)
        gate = value[:rows]
        extra = value[rows:]
        total = gate if total is None else total + gate
        squares = extra if squares is None else squares + extra
    columns = []
    if rows <= width:
        line = squares[0:1, :rows] + squares[1:2, :rows]
    else:
        line = jnp.concatenate(
            [squares[2 * i : 2 * i + 1] + squares[2 * i + 1 : 2 * i + 2] for i in range(rows // width)], axis=1
        )
    inverse = lax.rsqrt(line / features + 1e-06)
    column = jnp.transpose(jnp.broadcast_to(inverse, (8, rows)))[:, 0:1]
    gate = total * column
    out_ref[...] = (gate / (1.0 + jnp.exp(-gate))).astype(bf16)


def down_kernel(n_tensor, n, cap, block_ref, w_ref, *refs):
    pieces, outs = refs[:n_tensor], refs[n_tensor:]
    width = pieces[0].shape[1]
    total = None
    for k in range(n_tensor):
        start = pl.multiple_of((block_ref[0] ^ k) * width, width)
        term = jnp.dot(pieces[k][...], w_ref[0, pl.ds(start, width), :], preferred_element_type=jnp.float32)
        total = term if total is None else total + term
    for k in range(n):
        outs[k][...] = total[k * cap : (k + 1) * cap, :].astype(jnp.bfloat16)


def combine_kernel(n, high_ref, low_ref, *refs):
    pieces, out_ref = refs[:n], refs[n]
    rows = jnp.concatenate([p[...].astype(jnp.float32) for p in pieces], axis=0).astype(jnp.bfloat16)
    total = jnp.dot(high_ref[...], rows, preferred_element_type=jnp.float32)
    total += jnp.dot(low_ref[...], rows, preferred_element_type=jnp.float32)
    out_ref[...] = total.astype(jnp.bfloat16)


def local(residual, attn_partial, norm_gain, expert_ids, route_scores, w_gate, w_down):
    bf16, f32 = jnp.bfloat16, jnp.float32
    tokens, share = residual.shape
    nt, ne = lax.axis_size("tensor"), lax.axis_size("expert")
    z, me = lax.axis_index("tensor"), lax.axis_index("expert")
    top = expert_ids.shape[1]
    cap = tokens * top // ne * 5 // 4
    rows = ne * cap
    ff = w_gate.shape[2] // nt
    me_arr = jnp.full((1,), me, jnp.int32)
    z_arr = jnp.full((1,), z, jnp.int32)
    sds = jax.ShapeDtypeStruct

    parts = {}
    for k in partners(nt):
        block = lax.dynamic_slice(attn_partial[0], (0, (z ^ k) * share), (tokens, share))
        parts[k] = exchange(block, "tensor", k) if k else block

    select, high, low = pl.pallas_call(
        functools.partial(routing_kernel, ne, cap),
        out_shape=(sds((rows, tokens), bf16), sds((tokens, rows), bf16), sds((tokens, rows), bf16)),
        in_specs=[scalar(), whole(), whole(), whole()],
        out_specs=(whole(),) * 3,
        compiler_params=params(),
        name="routing",
    )(me_arr, expert_ids, expert_ids.T, route_scores)

    packed = pl.pallas_call(
        functools.partial(pack_kernel, nt, ne, cap),
        out_shape=(sds((tokens, share), bf16),) + (sds((cap, share), bf16),) * ne,
        in_specs=[whole()] * (2 + nt),
        out_specs=(whole(),) * (1 + ne),
        compiler_params=params(),
        name="pack",
    )(residual, select, *[parts[k] for k in range(nt)])
    stream, outgoing = packed[0], packed[1:]

    arrived = {}
    for k in partners(ne):
        arrived[k] = exchange(outgoing[k], "expert", k) if k else outgoing[k]

    lhs, squares = pl.pallas_call(
        functools.partial(prepare_kernel, ne),
        out_shape=(sds((rows, share), bf16), sds((8, rows), f32)),
        in_specs=[whole()] * (1 + ne),
        out_specs=(whole(),) * 2,
        compiler_params=params(),
        name="prepare",
    )(norm_gain[None, :], *[arrived[k] for k in range(ne)])

    tall = rows + extra_rows(rows, ff)
    gates = {}
    for k in partners(nt):
        partial_gate = pl.pallas_call(
            gate_kernel,
            out_shape=sds((tall, ff), bf16),
            grid_spec=pltpu.PrefetchScalarGridSpec(
                num_scalar_prefetch=1,
                grid=(1,),
                in_specs=[
                    pl.BlockSpec((rows, share), lambda i, b: (0, 0)),
                    pl.BlockSpec((8, rows), lambda i, b: (0, 0)),
                    pl.BlockSpec((1, share, ff), lambda i, b: (0, 0, b[0])),
                ],
                out_specs=pl.BlockSpec((tall, ff), lambda i, b: (0, 0)),
            ),
            compiler_params=params(),
            cost_estimate=pl.CostEstimate(
                flops=2 * rows * share * ff, bytes_accessed=2 * (share * ff + rows * share), transcendentals=0
            ),
            name="gate",
        )(z_arr ^ k, lhs, squares, w_gate)
        gates[k] = exchange(partial_gate, "tensor", k) if k else partial_gate

    hidden_own = pl.pallas_call(
        functools.partial(activate_kernel, nt, rows, float(share * nt)),
        out_shape=sds((rows, ff), bf16),
        in_specs=[whole()] * nt,
        out_specs=whole(),
        compiler_params=params(),
        name="activate",
    )(*[gates[k] for k in range(nt)])
    hidden = {}
    for k in partners(nt):
        hidden[k] = exchange(hidden_own, "tensor", k) if k else hidden_own

    produced = pl.pallas_call(
        functools.partial(down_kernel, nt, ne, cap),
        out_shape=(sds((cap, share), bf16),) * ne,
        in_specs=[scalar(), whole()] + [whole()] * nt,
        out_specs=(whole(),) * ne,
        compiler_params=params(),
        name="down",
    )(z_arr, w_down, *[hidden[k] for k in range(nt)])
    returned = {}
    for k in partners(ne):
        returned[k] = exchange(produced[k], "expert", k) if k else produced[k]

    moe_out = pl.pallas_call(
        functools.partial(combine_kernel, ne),
        out_shape=sds((tokens, share), bf16),
        in_specs=[whole()] * (2 + ne),
        out_specs=whole(),
        compiler_params=params(),
        name="combine",
    )(high, low, *[returned[k] for k in range(ne)])
    return stream, moe_out


def solution(mesh):
    return jax.shard_map(
        local,
        mesh=mesh,
        in_specs=(
            P(("groups", "expert"), "tensor"),
            P("tensor", ("groups", "expert"), None),
            P("tensor"),
            P(("groups", "expert"), None),
            P(("groups", "expert"), None),
            P("expert", "tensor", None),
            P("expert", None, "tensor"),
        ),
        out_specs=(P(("groups", "expert"), "tensor"), P(("groups", "expert"), "tensor")),
        check_vma=False,
    )
```

```python
import functools

import jax
import jax.numpy as jnp
from jax import lax
from jax.experimental import pallas as pl
from jax.experimental.pallas import tpu as pltpu
from jax.sharding import PartitionSpec as P


def partners(n):
    return list(range(n - 1, -1, -1))


def exchange(value, axis, step):
    n = lax.axis_size(axis)
    return lax.ppermute(value, axis, [(i, i ^ step) for i in range(n)])


def params(mib=16):
    return pltpu.CompilerParams(vmem_limit_bytes=mib << 20)


def whole():
    return pl.BlockSpec(memory_space=pltpu.VMEM)


def anywhere():
    return pl.BlockSpec(memory_space=pl.ANY)


def scalar():
    return pl.BlockSpec(memory_space=pltpu.SMEM)


def routing_kernel(n, cap, me_ref, ids_ref, idst_ref, scores_ref, select_ref, high_ref, low_ref):
    me = me_ref[0]
    tokens, top = ids_ref.shape
    f32, bf16 = jnp.float32, jnp.bfloat16
    row = lax.broadcasted_iota(jnp.int32, (tokens, tokens), 0)
    col = lax.broadcasted_iota(jnp.int32, (tokens, tokens), 1)
    before_t = jnp.where(row < col, 1.0, 0.0).astype(bf16)
    before = jnp.where(col < row, 1.0, 0.0).astype(bf16)
    scores = scores_ref[...]
    weights = 2.827 * scores / jnp.sum(scores, axis=1, keepdims=True)
    slot_t = lax.broadcasted_iota(jnp.int32, (cap, tokens), 0)
    slot = lax.broadcasted_iota(jnp.int32, (tokens, cap), 1)
    selects, highs, lows = [], [], []
    for k in range(n):
        expert = me ^ k
        named_t = jnp.zeros((1, tokens), f32)
        named = jnp.zeros((tokens, 1), f32)
        weight = jnp.zeros((tokens, 1), f32)
        for j in range(top):
            hit = jnp.where(ids_ref[:, j : j + 1] == expert, 1.0, 0.0)
            named_t += jnp.where(idst_ref[j : j + 1, :] == expert, 1.0, 0.0)
            named += hit
            weight += hit * weights[:, j : j + 1]
        place_t = jnp.dot(
            jnp.broadcast_to(named_t, (8, tokens)).astype(bf16), before_t, preferred_element_type=f32
        )[0:1, :].astype(jnp.int32)
        place = jnp.dot(
            before, jnp.broadcast_to(named, (tokens, 128)).astype(bf16), preferred_element_type=f32
        )[:, 0:1].astype(jnp.int32)
        selects.append(jnp.where(place_t == slot_t, jnp.broadcast_to(named_t, slot_t.shape), 0.0))
        full = jnp.where(place == slot, jnp.broadcast_to(weight, slot.shape), 0.0)
        high = full.astype(bf16).astype(f32)
        highs.append(high)
        lows.append(full - high)
    select_ref[...] = jnp.concatenate(selects, axis=0).astype(bf16)
    high_ref[...] = jnp.concatenate(highs, axis=1).astype(bf16)
    low_ref[...] = jnp.concatenate(lows, axis=1).astype(bf16)


def fetch_kernel(*refs):
    *pairs, sems = refs
    half = len(pairs) // 2
    copies = [pltpu.make_async_copy(pairs[i], pairs[half + i], sems.at[i]) for i in range(half)]
    for copy in copies:
        copy.start()
    for copy in copies:
        copy.wait()


def add_kernel(n_tensor, cap, ks, residual_ref, select_ref, *refs):
    parts, stream_ref, kept_ref, outs = refs[:n_tensor], *refs[n_tensor : n_tensor + 2], refs[n_tensor + 2 :]
    total = residual_ref[...].astype(jnp.float32)
    for part in parts:
        total += part[...].astype(jnp.float32)
    stream_ref[...] = total.astype(jnp.bfloat16)
    kept_ref[...] = total.astype(jnp.bfloat16)
    pack_kernel(cap, ks, kept_ref, select_ref, *outs)


def pack_kernel(cap, ks, stream_ref, select_ref, *outs):
    first, last = ks[0] * cap, (ks[-1] + 1) * cap
    packed = jnp.dot(select_ref[first:last, :], stream_ref[...], preferred_element_type=jnp.float32)
    for i, out in enumerate(outs):
        out[...] = packed[i * cap : (i + 1) * cap, :].astype(jnp.bfloat16)


def prepare_kernel(n, gain_ref, *refs):
    pieces, lhs_ref, squares_ref = refs[:n], refs[-2], refs[-1]
    rows = jnp.concatenate([p[...].astype(jnp.float32) for p in pieces], axis=0)
    squared = (rows * rows).astype(jnp.bfloat16)
    ones = jnp.ones((8, rows.shape[1]), jnp.bfloat16)
    sums = lax.dot_general(ones, squared, (((1,), (1,)), ((), ())), preferred_element_type=jnp.float32)
    high = sums.astype(jnp.bfloat16).astype(jnp.float32)
    low = sums - high
    which = lax.broadcasted_iota(jnp.int32, sums.shape, 0)
    squares_ref[...] = jnp.where(which == 0, high, jnp.where(which == 1, low, 0.0))
    lhs_ref[...] = (rows * gain_ref[...].astype(jnp.float32)).astype(jnp.bfloat16)


def extra_rows(rows, width):
    return -(-2 * -(-rows // width) // 8) * 8


def gate_kernel(block_ref, lhs_ref, squares_ref, w_ref, *refs):
    out_ref = refs[-1]
    rows = lhs_ref.shape[0]
    width = out_ref.shape[1]
    extra = extra_rows(rows, width)
    product = jnp.dot(lhs_ref[...], w_ref[0], preferred_element_type=jnp.float32)
    squares = squares_ref[...]
    pieces = -(-rows // width)
    if rows % width:
        squares = jnp.concatenate([squares, jnp.zeros((8, width - rows % width), jnp.float32)], axis=1)
    if pieces == 1:
        below = squares
    else:
        below = jnp.concatenate(
            [squares[0:2, i * width : (i + 1) * width] for i in range(pieces)]
            + ([jnp.zeros((extra - 2 * pieces, width), jnp.float32)] if extra > 2 * pieces else []),
            axis=0,
        )
    out_ref[...] = jnp.concatenate([product, below], axis=0).astype(jnp.bfloat16)


def activate_kernel(n, rows, features, *refs):
    parts, out_ref = refs[:n], refs[-1]
    f32, bf16 = jnp.float32, jnp.bfloat16
    width = out_ref.shape[1]
    total, squares = None, None
    for part in parts:
        value = part[...].astype(f32)
        gate = value[:rows]
        extra = value[rows:]
        total = gate if total is None else total + gate
        squares = extra if squares is None else squares + extra
    pieces = -(-rows // width)
    lines = [squares[2 * i : 2 * i + 1] + squares[2 * i + 1 : 2 * i + 2] for i in range(pieces)]
    line = (lines[0] if pieces == 1 else jnp.concatenate(lines, axis=1))[:, :rows]
    inverse = lax.rsqrt(line / features + 1e-06)
    column = jnp.transpose(jnp.broadcast_to(inverse, (8, rows)))[:, 0:1]
    gate = total * column
    out_ref[...] = (gate / (1.0 + jnp.exp(-gate))).astype(bf16)


def down_kernel(n_tensor, n, cap, block_ref, w_ref, *refs):
    pieces, outs = refs[:n_tensor], refs[n_tensor:]
    width = pieces[0].shape[1]
    total = None
    for k in range(n_tensor):
        start = pl.multiple_of((block_ref[0] ^ k) * width, width)
        term = jnp.dot(pieces[k][...], w_ref[0, pl.ds(start, width), :], preferred_element_type=jnp.float32)
        total = term if total is None else total + term
    for k in range(n):
        outs[k][...] = total[k * cap : (k + 1) * cap, :].astype(jnp.bfloat16)


def combine_kernel(n, high_ref, low_ref, *refs):
    pieces, out_ref = refs[:n], refs[n]
    rows = jnp.concatenate([p[...].astype(jnp.float32) for p in pieces], axis=0).astype(jnp.bfloat16)
    total = jnp.dot(high_ref[...], rows, preferred_element_type=jnp.float32)
    total += jnp.dot(low_ref[...], rows, preferred_element_type=jnp.float32)
    out_ref[...] = total.astype(jnp.bfloat16)


def estimate(flops, moved):
    return pl.CostEstimate(flops=int(flops), bytes_accessed=int(moved), transcendentals=0)


def local(residual, attn_partial, norm_gain, expert_ids, route_scores, w_gate, w_down):
    bf16, f32 = jnp.bfloat16, jnp.float32
    tokens, share = residual.shape
    nt, ne = lax.axis_size("tensor"), lax.axis_size("expert")
    z, me = lax.axis_index("tensor"), lax.axis_index("expert")
    top = expert_ids.shape[1]
    cap = tokens * top // ne * 5 // 4
    rows = ne * cap
    ff = w_gate.shape[2] // nt
    me_arr = jnp.full((1,), me, jnp.int32)
    z_arr = jnp.full((1,), z, jnp.int32)
    sds = jax.ShapeDtypeStruct
    near, far = [0, 1], list(range(2, ne))

    parts = {}
    for k in partners(nt):
        block = lax.dynamic_slice(attn_partial[0], (0, (z ^ k) * share), (tokens, share))
        parts[k] = exchange(block, "tensor", k) if k else block

    select, high, low = pl.pallas_call(
        functools.partial(routing_kernel, ne, cap),
        out_shape=(sds((rows, tokens), bf16), sds((tokens, rows), bf16), sds((tokens, rows), bf16)),
        in_specs=[scalar(), whole(), whole(), whole()],
        out_specs=(whole(),) * 3,
        compiler_params=params(),
        cost_estimate=estimate(10**6, 2**16),
        name="routing",
    )(me_arr, expert_ids, expert_ids.T, route_scores)

    fetched = (residual, w_gate)
    residual, w_gate = pl.pallas_call(
        fetch_kernel,
        out_shape=tuple(sds(v.shape, v.dtype) for v in fetched),
        in_specs=[anywhere()] * len(fetched),
        out_specs=(whole(),) * len(fetched),
        scratch_shapes=[pltpu.SemaphoreType.DMA((len(fetched),))],
        compiler_params=params(),
        cost_estimate=estimate(10**6, sum(2 * v.size for v in fetched)),
        name="fetch",
    )(*fetched)

    stream, kept, *near_rows = pl.pallas_call(
        functools.partial(add_kernel, nt, cap, near),
        out_shape=(sds((tokens, share), bf16),) * 2 + (sds((cap, share), bf16),) * len(near),
        in_specs=[whole()] * (2 + nt),
        out_specs=(whole(),) * (2 + len(near)),
        compiler_params=params(),
        cost_estimate=estimate(2 * rows * tokens * share, 4 * tokens * share * nt),
        name="add",
    )(residual, select, *[parts[k] for k in range(nt)])
    arrived = {0: near_rows[0], 1: exchange(near_rows[1], "expert", 1)}
    far_rows = pl.pallas_call(
        functools.partial(pack_kernel, cap, far),
        out_shape=(sds((cap, share), bf16),) * len(far),
        in_specs=[whole()] * 2,
        out_specs=(whole(),) * len(far),
        compiler_params=params(),
        cost_estimate=estimate(2 * rows * tokens * share, 4 * tokens * share),
        name="pack",
    )(kept, select)
    for k, value in zip(far, far_rows):
        arrived[k] = exchange(value, "expert", k)

    def summed_gate(ks, after=None):
        count = len(ks) * cap
        lhs, squares = pl.pallas_call(
            functools.partial(prepare_kernel, len(ks)),
            out_shape=(sds((count, share), bf16), sds((8, count), f32)),
            in_specs=[whole()] * (1 + len(ks)),
            out_specs=(whole(),) * 2,
            compiler_params=params(),
            cost_estimate=estimate(16 * count * share, 4 * count * share),
            name="prepare",
        )(norm_gain[None, :], *[arrived[k] for k in ks])
        tall = count + extra_rows(count, ff)
        gates = {}
        for k in partners(nt):
            earlier = [] if after is None else [after[k or 1]]
            partial_gate = pl.pallas_call(
                gate_kernel,
                out_shape=sds((tall, ff), bf16),
                grid_spec=pltpu.PrefetchScalarGridSpec(
                    num_scalar_prefetch=1,
                    grid=(1,),
                    in_specs=[
                        pl.BlockSpec((count, share), lambda i, b: (0, 0)),
                        pl.BlockSpec((8, count), lambda i, b: (0, 0)),
                        pl.BlockSpec((1, share, ff), lambda i, b: (0, 0, b[0])),
                    ]
                    + [anywhere()] * len(earlier),
                    out_specs=pl.BlockSpec((tall, ff), lambda i, b: (0, 0)),
                ),
                compiler_params=params(),
                cost_estimate=estimate(2 * count * share * ff, 2 * share * ff),
                name="gate",
            )(z_arr ^ k, lhs, squares, w_gate, *earlier)
            gates[k] = exchange(partial_gate, "tensor", k) if k else partial_gate
        return gates

    def gathered_hidden(ks, gates, after=()):
        count = len(ks) * cap
        own = pl.pallas_call(
            functools.partial(activate_kernel, nt, count, float(share * nt)),
            out_shape=sds((count, ff), bf16),
            in_specs=[whole()] * nt + [anywhere()] * len(after),
            out_specs=whole(),
            compiler_params=params(),
            cost_estimate=estimate(20 * count * ff, 2 * count * ff * (nt + 1)),
            name="activate",
        )(*[gates[k] for k in range(nt)], *after)
        return {k: exchange(own, "tensor", k) if k else own for k in partners(nt)}

    def produced(ks, hidden):
        outs = pl.pallas_call(
            functools.partial(down_kernel, nt, len(ks), cap),
            out_shape=(sds((cap, share), bf16),) * len(ks),
            in_specs=[scalar(), whole()] + [whole()] * nt,
            out_specs=(whole(),) * len(ks),
            compiler_params=params(),
            cost_estimate=estimate(2 * len(ks) * cap * share * ff * nt, 2 * share * ff * nt),
            name="down",
        )(z_arr, w_down, *[hidden[k] for k in range(nt)])
        return dict(zip(ks, outs))

    near_gates = summed_gate(near)
    far_gates = summed_gate(far, near_gates)
    far_hidden = gathered_hidden(far, far_gates)
    near_hidden = gathered_hidden(near, near_gates, (far_hidden[3],))
    returned = {}
    for ks, hidden in ((far, far_hidden), (near, near_hidden)):
        for k, value in produced(ks, hidden).items():
            returned[k] = exchange(value, "expert", k) if k else value

    moe_out = pl.pallas_call(
        functools.partial(combine_kernel, ne),
        out_shape=sds((tokens, share), bf16),
        in_specs=[whole()] * (2 + ne),
        out_specs=whole(),
        compiler_params=params(),
        cost_estimate=estimate(4 * rows * tokens * share, 2 * rows * share),
        name="combine",
    )(high, low, *[returned[k] for k in range(ne)])
    return stream, moe_out


def solution(mesh):
    return jax.shard_map(
        local,
        mesh=mesh,
        in_specs=(
            P(("groups", "expert"), "tensor"),
            P("tensor", ("groups", "expert"), None),
            P("tensor"),
            P(("groups", "expert"), None),
            P(("groups", "expert"), None),
            P("expert", "tensor", None),
            P("expert", None, "tensor"),
        ),
        out_specs=(P(("groups", "expert"), "tensor"), P(("groups", "expert"), "tensor")),
        check_vma=False,
    )
```

```python
import functools

import jax
import jax.numpy as jnp
from jax import lax
from jax.experimental import pallas as pl
from jax.experimental.pallas import tpu as pltpu
from jax.sharding import PartitionSpec as P


def partners(n):
    return list(range(n - 1, -1, -1))


def exchange(value, axis, step):
    n = lax.axis_size(axis)
    return lax.ppermute(value, axis, [(i, i ^ step) for i in range(n)])


def params(mib=16):
    return pltpu.CompilerParams(vmem_limit_bytes=mib << 20)


def whole():
    return pl.BlockSpec(memory_space=pltpu.VMEM)


def anywhere():
    return pl.BlockSpec(memory_space=pl.ANY)


def scalar():
    return pl.BlockSpec(memory_space=pltpu.SMEM)


def routing_kernel(n, cap, me_ref, ids_ref, idst_ref, scores_ref, select_ref, high_ref, low_ref):
    me = me_ref[0]
    tokens, top = ids_ref.shape
    f32, bf16 = jnp.float32, jnp.bfloat16
    row = lax.broadcasted_iota(jnp.int32, (tokens, tokens), 0)
    col = lax.broadcasted_iota(jnp.int32, (tokens, tokens), 1)
    before_t = jnp.where(row < col, 1.0, 0.0).astype(bf16)
    before = jnp.where(col < row, 1.0, 0.0).astype(bf16)
    scores = scores_ref[...]
    weights = 2.827 * scores / jnp.sum(scores, axis=1, keepdims=True)
    slot_t = lax.broadcasted_iota(jnp.int32, (cap, tokens), 0)
    slot = lax.broadcasted_iota(jnp.int32, (tokens, cap), 1)
    selects, highs, lows = [], [], []
    for k in range(n):
        expert = me ^ k
        named_t = jnp.zeros((1, tokens), f32)
        named = jnp.zeros((tokens, 1), f32)
        weight = jnp.zeros((tokens, 1), f32)
        for j in range(top):
            hit = jnp.where(ids_ref[:, j : j + 1] == expert, 1.0, 0.0)
            named_t += jnp.where(idst_ref[j : j + 1, :] == expert, 1.0, 0.0)
            named += hit
            weight += hit * weights[:, j : j + 1]
        place_t = jnp.dot(
            jnp.broadcast_to(named_t, (8, tokens)).astype(bf16), before_t, preferred_element_type=f32
        )[0:1, :].astype(jnp.int32)
        place = jnp.dot(
            before, jnp.broadcast_to(named, (tokens, 128)).astype(bf16), preferred_element_type=f32
        )[:, 0:1].astype(jnp.int32)
        selects.append(jnp.where(place_t == slot_t, jnp.broadcast_to(named_t, slot_t.shape), 0.0))
        full = jnp.where(place == slot, jnp.broadcast_to(weight, slot.shape), 0.0)
        high = full.astype(bf16).astype(f32)
        highs.append(high)
        lows.append(full - high)
    select_ref[...] = jnp.concatenate(selects, axis=0).astype(bf16)
    high_ref[...] = jnp.concatenate(highs, axis=1).astype(bf16)
    low_ref[...] = jnp.concatenate(lows, axis=1).astype(bf16)


def fetch_kernel(*refs):
    *pairs, sems = refs
    half = len(pairs) // 2
    copies = [pltpu.make_async_copy(pairs[i], pairs[half + i], sems.at[i]) for i in range(half)]
    for copy in copies:
        copy.start()
    for copy in copies:
        copy.wait()


def merge_kernel(end_ref, own_ref, passing_ref, relayed_ref, out_ref):
    @pl.when(end_ref[0] == 1)
    def _():
        out_ref[...] = own_ref[...]

    @pl.when(end_ref[0] == 0)
    def _():
        total = passing_ref[...].astype(jnp.float32) + relayed_ref[...].astype(jnp.float32)
        out_ref[...] = total.astype(jnp.bfloat16)


def add_kernel(n_tensor, cap, ks, last_ref, residual_ref, select_ref, *refs):
    parts, stream_ref, kept_ref, outs = refs[:n_tensor], *refs[n_tensor : n_tensor + 2], refs[n_tensor + 2 :]
    total = residual_ref[...].astype(jnp.float32)
    for part in parts[:-1]:
        total += part[...].astype(jnp.float32)
    total += jnp.where(last_ref[0] == 1, parts[-1][...].astype(jnp.float32), 0.0)
    stream_ref[...] = total.astype(jnp.bfloat16)
    kept_ref[...] = total.astype(jnp.bfloat16)
    pack_kernel(cap, ks, kept_ref, select_ref, *outs)


def pack_kernel(cap, ks, stream_ref, select_ref, *outs):
    first, last = ks[0] * cap, (ks[-1] + 1) * cap
    packed = jnp.dot(select_ref[first:last, :], stream_ref[...], preferred_element_type=jnp.float32)
    for i, out in enumerate(outs):
        out[...] = packed[i * cap : (i + 1) * cap, :].astype(jnp.bfloat16)


def prepare_kernel(n, gain_ref, *refs):
    pieces, lhs_ref, squares_ref = refs[:n], refs[-2], refs[-1]
    rows = jnp.concatenate([p[...].astype(jnp.float32) for p in pieces], axis=0)
    squared = (rows * rows).astype(jnp.bfloat16)
    ones = jnp.ones((8, rows.shape[1]), jnp.bfloat16)
    sums = lax.dot_general(ones, squared, (((1,), (1,)), ((), ())), preferred_element_type=jnp.float32)
    high = sums.astype(jnp.bfloat16).astype(jnp.float32)
    low = sums - high
    which = lax.broadcasted_iota(jnp.int32, sums.shape, 0)
    squares_ref[...] = jnp.where(which == 0, high, jnp.where(which == 1, low, 0.0))
    lhs_ref[...] = (rows * gain_ref[...].astype(jnp.float32)).astype(jnp.bfloat16)


def extra_rows(rows, width):
    return -(-2 * -(-rows // width) // 8) * 8


def gate_kernel(block_ref, lhs_ref, squares_ref, w_ref, *refs):
    out_ref = refs[-1]
    rows = lhs_ref.shape[0]
    width = out_ref.shape[1]
    extra = extra_rows(rows, width)
    product = jnp.dot(lhs_ref[...], w_ref[0], preferred_element_type=jnp.float32)
    squares = squares_ref[...]
    pieces = -(-rows // width)
    if rows % width:
        squares = jnp.concatenate([squares, jnp.zeros((8, width - rows % width), jnp.float32)], axis=1)
    if pieces == 1:
        below = squares
    else:
        below = jnp.concatenate(
            [squares[0:2, i * width : (i + 1) * width] for i in range(pieces)]
            + ([jnp.zeros((extra - 2 * pieces, width), jnp.float32)] if extra > 2 * pieces else []),
            axis=0,
        )
    out_ref[...] = jnp.concatenate([product, below], axis=0).astype(jnp.bfloat16)


def activate_kernel(n, rows, features, *refs):
    parts, out_ref = refs[:n], refs[-1]
    f32, bf16 = jnp.float32, jnp.bfloat16
    width = out_ref.shape[1]
    total, squares = None, None
    for part in parts:
        value = part[...].astype(f32)
        gate = value[:rows]
        extra = value[rows:]
        total = gate if total is None else total + gate
        squares = extra if squares is None else squares + extra
    pieces = -(-rows // width)
    lines = [squares[2 * i : 2 * i + 1] + squares[2 * i + 1 : 2 * i + 2] for i in range(pieces)]
    line = (lines[0] if pieces == 1 else jnp.concatenate(lines, axis=1))[:, :rows]
    inverse = lax.rsqrt(line / features + 1e-06)
    column = jnp.transpose(jnp.broadcast_to(inverse, (8, rows)))[:, 0:1]
    gate = total * column
    out_ref[...] = (gate / (1.0 + jnp.exp(-gate))).astype(bf16)


def down_kernel(n_tensor, n, cap, block_ref, w_ref, *refs):
    pieces, outs = refs[:n_tensor], refs[n_tensor:]
    width = pieces[0].shape[1]
    total = None
    for i, k in enumerate(partners(n_tensor)):
        start = pl.multiple_of((block_ref[0] ^ k) * width, width)
        term = jnp.dot(pieces[i][...], w_ref[0, pl.ds(start, width), :], preferred_element_type=jnp.float32)
        total = term if total is None else total + term
    for k in range(n):
        outs[k][...] = total[k * cap : (k + 1) * cap, :].astype(jnp.bfloat16)


def combine_kernel(n, high_ref, low_ref, *refs):
    pieces, out_ref = refs[:n], refs[n]
    rows = jnp.concatenate([p[...].astype(jnp.float32) for p in pieces], axis=0).astype(jnp.bfloat16)
    total = jnp.dot(high_ref[...], rows, preferred_element_type=jnp.float32)
    total += jnp.dot(low_ref[...], rows, preferred_element_type=jnp.float32)
    out_ref[...] = total.astype(jnp.bfloat16)


def estimate(flops, moved):
    return pl.CostEstimate(flops=int(flops), bytes_accessed=int(moved), transcendentals=0)


def local(residual, attn_partial, norm_gain, expert_ids, route_scores, w_gate, w_down):
    bf16, f32 = jnp.bfloat16, jnp.float32
    tokens, share = residual.shape
    nt, ne = lax.axis_size("tensor"), lax.axis_size("expert")
    z, me = lax.axis_index("tensor"), lax.axis_index("expert")
    top = expert_ids.shape[1]
    cap = tokens * top // ne * 5 // 4
    rows = ne * cap
    ff = w_gate.shape[2] // nt
    me_arr = jnp.full((1,), me, jnp.int32)
    z_arr = jnp.full((1,), z, jnp.int32)
    sds = jax.ShapeDtypeStruct
    near, far = [0, 1], list(range(2, ne))

    def block(k):
        return lax.dynamic_slice(attn_partial[0], (0, k * share), (tokens, share))

    if nt == 4:
        end = (z == 0) | (z == 3)
        end_arr = jnp.where(end, 1, 0).astype(jnp.int32).reshape(1)
        relayed = exchange(block(jnp.where(end, z ^ 3, z ^ 1)), "tensor", 1)
        parts = [block(z)]
        parts.append(lax.ppermute(block(z ^ 3), "tensor", [(1, 2), (2, 1)]))
        parts.append(lax.ppermute(block(z ^ 2), "tensor", [(0, 2), (3, 1)]))
        merged = pl.pallas_call(
            merge_kernel,
            out_shape=sds((tokens, share), bf16),
            in_specs=[scalar()] + [whole()] * 3,
            out_specs=whole(),
            compiler_params=params(),
            cost_estimate=estimate(2 * tokens * share, 8 * tokens * share),
            name="merge",
        )(end_arr, block(z ^ 1), block(z ^ 2), relayed)
        parts.append(lax.ppermute(merged, "tensor", [(0, 1), (1, 3), (2, 0), (3, 2)]))
        parts.append(relayed)
    else:
        end_arr = jnp.ones((1,), jnp.int32)
        parts = [exchange(block(z ^ k), "tensor", k) if k else block(z) for k in partners(nt)]

    select, high, low = pl.pallas_call(
        functools.partial(routing_kernel, ne, cap),
        out_shape=(sds((rows, tokens), bf16), sds((tokens, rows), bf16), sds((tokens, rows), bf16)),
        in_specs=[scalar(), whole(), whole(), whole()],
        out_specs=(whole(),) * 3,
        compiler_params=params(),
        cost_estimate=estimate(10**6, 2**16),
        name="routing",
    )(me_arr, expert_ids, expert_ids.T, route_scores)

    fetched = (residual, w_gate)
    residual, w_gate = pl.pallas_call(
        fetch_kernel,
        out_shape=tuple(sds(v.shape, v.dtype) for v in fetched),
        in_specs=[anywhere()] * len(fetched),
        out_specs=(whole(),) * len(fetched),
        scratch_shapes=[pltpu.SemaphoreType.DMA((len(fetched),))],
        compiler_params=params(),
        cost_estimate=estimate(10**6, sum(2 * v.size for v in fetched)),
        name="fetch",
    )(*fetched)

    stream, kept, *near_rows = pl.pallas_call(
        functools.partial(add_kernel, len(parts), cap, near),
        out_shape=(sds((tokens, share), bf16),) * 2 + (sds((cap, share), bf16),) * len(near),
        in_specs=[scalar()] + [whole()] * (2 + len(parts)),
        out_specs=(whole(),) * (2 + len(near)),
        compiler_params=params(),
        cost_estimate=estimate(2 * rows * tokens * share, 4 * tokens * share * nt),
        name="add",
    )(end_arr, residual, select, *parts)
    arrived = {0: near_rows[0], 1: exchange(near_rows[1], "expert", 1)}
    far_rows = pl.pallas_call(
        functools.partial(pack_kernel, cap, far),
        out_shape=(sds((cap, share), bf16),) * len(far),
        in_specs=[whole()] * 2,
        out_specs=(whole(),) * len(far),
        compiler_params=params(),
        cost_estimate=estimate(2 * rows * tokens * share, 4 * tokens * share),
        name="pack",
    )(kept, select)
    for k, value in zip(far, far_rows):
        arrived[k] = exchange(value, "expert", k)

    def summed_gate(ks, after=None):
        count = len(ks) * cap
        lhs, squares = pl.pallas_call(
            functools.partial(prepare_kernel, len(ks)),
            out_shape=(sds((count, share), bf16), sds((8, count), f32)),
            in_specs=[whole()] * (1 + len(ks)),
            out_specs=(whole(),) * 2,
            compiler_params=params(),
            cost_estimate=estimate(16 * count * share, 4 * count * share),
            name="prepare",
        )(norm_gain[None, :], *[arrived[k] for k in ks])
        tall = count + extra_rows(count, ff)
        gates = {}
        for k in partners(nt):
            earlier = [] if after is None else [after[k or 1]]
            partial_gate = pl.pallas_call(
                gate_kernel,
                out_shape=sds((tall, ff), bf16),
                grid_spec=pltpu.PrefetchScalarGridSpec(
                    num_scalar_prefetch=1,
                    grid=(1,),
                    in_specs=[
                        pl.BlockSpec((count, share), lambda i, b: (0, 0)),
                        pl.BlockSpec((8, count), lambda i, b: (0, 0)),
                        pl.BlockSpec((1, share, ff), lambda i, b: (0, 0, b[0])),
                    ]
                    + [anywhere()] * len(earlier),
                    out_specs=pl.BlockSpec((tall, ff), lambda i, b: (0, 0)),
                ),
                compiler_params=params(),
                cost_estimate=estimate(2 * count * share * ff, 2 * share * ff),
                name="gate",
            )(z_arr ^ k, lhs, squares, w_gate, *earlier)
            gates[k] = exchange(partial_gate, "tensor", k) if k else partial_gate
        return gates

    def gathered_hidden(ks, gates, after=()):
        count = len(ks) * cap
        own = pl.pallas_call(
            functools.partial(activate_kernel, nt, count, float(share * nt)),
            out_shape=sds((count, ff), bf16),
            in_specs=[whole()] * nt + [anywhere()] * len(after),
            out_specs=whole(),
            compiler_params=params(),
            cost_estimate=estimate(20 * count * ff, 2 * count * ff * (nt + 1)),
            name="activate",
        )(*[gates[k] for k in range(nt)], *after)
        return {k: exchange(own, "tensor", k) if k else own for k in partners(nt)}

    def produced(ks, hidden):
        outs = pl.pallas_call(
            functools.partial(down_kernel, nt, len(ks), cap),
            out_shape=(sds((cap, share), bf16),) * len(ks),
            in_specs=[scalar(), whole()] + [whole()] * nt,
            out_specs=(whole(),) * len(ks),
            compiler_params=params(),
            cost_estimate=estimate(2 * len(ks) * cap * share * ff * nt, 2 * share * ff * nt),
            name="down",
        )(z_arr, w_down, *[hidden[k] for k in partners(nt)])
        return dict(zip(ks, outs))

    near_gates = summed_gate(near)
    far_gates = summed_gate(far, near_gates)
    far_hidden = gathered_hidden(far, far_gates)
    near_hidden = gathered_hidden(near, near_gates, (far_hidden[3],))
    returned = {}
    for ks, hidden in ((far, far_hidden), (near, near_hidden)):
        for k, value in produced(ks, hidden).items():
            returned[k] = exchange(value, "expert", k) if k else value

    moe_out = pl.pallas_call(
        functools.partial(combine_kernel, ne),
        out_shape=sds((tokens, share), bf16),
        in_specs=[whole()] * (2 + ne),
        out_specs=whole(),
        compiler_params=params(),
        cost_estimate=estimate(4 * rows * tokens * share, 2 * rows * share),
        name="combine",
    )(high, low, *[returned[k] for k in range(ne)])
    return stream, moe_out


def solution(mesh):
    return jax.shard_map(
        local,
        mesh=mesh,
        in_specs=(
            P(("groups", "expert"), "tensor"),
            P("tensor", ("groups", "expert"), None),
            P("tensor"),
            P(("groups", "expert"), None),
            P(("groups", "expert"), None),
            P("expert", "tensor", None),
            P("expert", None, "tensor"),
        ),
        out_specs=(P(("groups", "expert"), "tensor"), P(("groups", "expert"), "tensor")),
        check_vma=False,
    )
```

```python
import functools

import jax
import jax.numpy as jnp
from jax import lax
from jax.experimental import pallas as pl
from jax.experimental.pallas import tpu as pltpu
from jax.sharding import PartitionSpec as P


def partners(n):
    return list(range(n - 1, -1, -1))


def exchange(value, axis, step):
    n = lax.axis_size(axis)
    return lax.ppermute(value, axis, [(i, i ^ step) for i in range(n)])


def params(mib=16):
    return pltpu.CompilerParams(vmem_limit_bytes=mib << 20)


def whole():
    return pl.BlockSpec(memory_space=pltpu.VMEM)


def anywhere():
    return pl.BlockSpec(memory_space=pl.ANY)


def scalar():
    return pl.BlockSpec(memory_space=pltpu.SMEM)


def routing_kernel(n, cap, me_ref, ids_ref, idst_ref, scores_ref, select_ref, high_ref, low_ref):
    me = me_ref[0]
    tokens, top = ids_ref.shape
    f32, bf16 = jnp.float32, jnp.bfloat16
    row = lax.broadcasted_iota(jnp.int32, (tokens, tokens), 0)
    col = lax.broadcasted_iota(jnp.int32, (tokens, tokens), 1)
    before_t = jnp.where(row < col, 1.0, 0.0).astype(bf16)
    before = jnp.where(col < row, 1.0, 0.0).astype(bf16)
    scores = scores_ref[...]
    weights = 2.827 * scores / jnp.sum(scores, axis=1, keepdims=True)
    slot_t = lax.broadcasted_iota(jnp.int32, (cap, tokens), 0)
    slot = lax.broadcasted_iota(jnp.int32, (tokens, cap), 1)
    selects, highs, lows = [], [], []
    for k in range(n):
        expert = me ^ k
        named_t = jnp.zeros((1, tokens), f32)
        named = jnp.zeros((tokens, 1), f32)
        weight = jnp.zeros((tokens, 1), f32)
        for j in range(top):
            hit = jnp.where(ids_ref[:, j : j + 1] == expert, 1.0, 0.0)
            named_t += jnp.where(idst_ref[j : j + 1, :] == expert, 1.0, 0.0)
            named += hit
            weight += hit * weights[:, j : j + 1]
        place_t = jnp.dot(
            jnp.broadcast_to(named_t, (8, tokens)).astype(bf16), before_t, preferred_element_type=f32
        )[0:1, :].astype(jnp.int32)
        place = jnp.dot(
            before, jnp.broadcast_to(named, (tokens, 128)).astype(bf16), preferred_element_type=f32
        )[:, 0:1].astype(jnp.int32)
        selects.append(jnp.where(place_t == slot_t, jnp.broadcast_to(named_t, slot_t.shape), 0.0))
        full = jnp.where(place == slot, jnp.broadcast_to(weight, slot.shape), 0.0)
        high = full.astype(bf16).astype(f32)
        highs.append(high)
        lows.append(full - high)
    select_ref[...] = jnp.concatenate(selects, axis=0).astype(bf16)
    high_ref[...] = jnp.concatenate(highs, axis=1).astype(bf16)
    low_ref[...] = jnp.concatenate(lows, axis=1).astype(bf16)


def fetch_kernel(*refs):
    *pairs, sems = refs
    half = len(pairs) // 2
    copies = [pltpu.make_async_copy(pairs[i], pairs[half + i], sems.at[i]) for i in range(half)]
    for copy in copies:
        copy.start()
    for copy in copies:
        copy.wait()


def merge_kernel(end_ref, own_ref, passing_ref, relayed_ref, out_ref):
    @pl.when(end_ref[0] == 1)
    def _():
        out_ref[...] = own_ref[...]

    @pl.when(end_ref[0] == 0)
    def _():
        total = passing_ref[...].astype(jnp.float32) + relayed_ref[...].astype(jnp.float32)
        out_ref[...] = total.astype(jnp.bfloat16)


def add_kernel(n_tensor, cap, ks, last_ref, residual_ref, select_ref, *refs):
    parts, kept_ref, outs = refs[:n_tensor], refs[n_tensor], refs[n_tensor + 1 :]
    total = residual_ref[...].astype(jnp.float32)
    for part in parts[:-1]:
        total += part[...].astype(jnp.float32)
    total += jnp.where(last_ref[0] == 1, parts[-1][...].astype(jnp.float32), 0.0)
    kept_ref[...] = total.astype(jnp.bfloat16)
    pack_kernel(cap, ks, kept_ref, select_ref, *outs)


def pack_kernel(cap, ks, stream_ref, select_ref, *outs):
    first, last = ks[0] * cap, (ks[-1] + 1) * cap
    packed = jnp.dot(select_ref[first:last, :], stream_ref[...], preferred_element_type=jnp.float32)
    for i, out in enumerate(outs):
        out[...] = packed[i * cap : (i + 1) * cap, :].astype(jnp.bfloat16)


def store_kernel(values_ref, after_ref, out_ref):
    out_ref[...] = values_ref[...]


def prepare_kernel(n, gain_ref, *refs):
    pieces, lhs_ref, squares_ref = refs[:n], refs[-2], refs[-1]
    rows = jnp.concatenate([p[...].astype(jnp.float32) for p in pieces], axis=0)
    squared = (rows * rows).astype(jnp.bfloat16)
    ones = jnp.ones((8, rows.shape[1]), jnp.bfloat16)
    sums = lax.dot_general(ones, squared, (((1,), (1,)), ((), ())), preferred_element_type=jnp.float32)
    high = sums.astype(jnp.bfloat16).astype(jnp.float32)
    low = sums - high
    which = lax.broadcasted_iota(jnp.int32, sums.shape, 0)
    squares_ref[...] = jnp.where(which == 0, high, jnp.where(which == 1, low, 0.0))
    lhs_ref[...] = (rows * gain_ref[...].astype(jnp.float32)).astype(jnp.bfloat16)


def extra_rows(rows, width):
    return -(-2 * -(-rows // width) // 8) * 8


def gate_kernel(block_ref, lhs_ref, squares_ref, w_ref, *refs):
    out_ref = refs[-1]
    rows = lhs_ref.shape[0]
    width = out_ref.shape[1]
    extra = extra_rows(rows, width)
    product = jnp.dot(lhs_ref[...], w_ref[0], preferred_element_type=jnp.float32)
    squares = squares_ref[...]
    pieces = -(-rows // width)
    if rows % width:
        squares = jnp.concatenate([squares, jnp.zeros((8, width - rows % width), jnp.float32)], axis=1)
    if pieces == 1:
        below = squares
    else:
        below = jnp.concatenate(
            [squares[0:2, i * width : (i + 1) * width] for i in range(pieces)]
            + ([jnp.zeros((extra - 2 * pieces, width), jnp.float32)] if extra > 2 * pieces else []),
            axis=0,
        )
    out_ref[...] = jnp.concatenate([product, below], axis=0).astype(jnp.bfloat16)


def activate_kernel(n, rows, features, *refs):
    parts, out_ref = refs[:n], refs[-1]
    f32, bf16 = jnp.float32, jnp.bfloat16
    width = out_ref.shape[1]
    total, squares = None, None
    for part in parts:
        value = part[...].astype(f32)
        gate = value[:rows]
        extra = value[rows:]
        total = gate if total is None else total + gate
        squares = extra if squares is None else squares + extra
    pieces = -(-rows // width)
    lines = [squares[2 * i : 2 * i + 1] + squares[2 * i + 1 : 2 * i + 2] for i in range(pieces)]
    line = (lines[0] if pieces == 1 else jnp.concatenate(lines, axis=1))[:, :rows]
    inverse = lax.rsqrt(line / features + 1e-06)
    column = jnp.transpose(jnp.broadcast_to(inverse, (8, rows)))[:, 0:1]
    gate = total * column
    out_ref[...] = (gate / (1.0 + jnp.exp(-gate))).astype(bf16)


def down_kernel(n_tensor, n, cap, block_ref, w_ref, *refs):
    pieces, outs = refs[:n_tensor], refs[n_tensor:]
    width = pieces[0].shape[1]
    total = None
    for i, k in enumerate(partners(n_tensor)):
        start = pl.multiple_of((block_ref[0] ^ k) * width, width)
        term = jnp.dot(pieces[i][...], w_ref[0, pl.ds(start, width), :], preferred_element_type=jnp.float32)
        total = term if total is None else total + term
    for k in range(n):
        outs[k][...] = total[k * cap : (k + 1) * cap, :].astype(jnp.bfloat16)


def combine_kernel(n, high_ref, low_ref, *refs):
    pieces, out_ref = refs[:n], refs[n]
    rows = jnp.concatenate([p[...].astype(jnp.float32) for p in pieces], axis=0).astype(jnp.bfloat16)
    total = jnp.dot(high_ref[...], rows, preferred_element_type=jnp.float32)
    total += jnp.dot(low_ref[...], rows, preferred_element_type=jnp.float32)
    out_ref[...] = total.astype(jnp.bfloat16)


def estimate(flops, moved):
    return pl.CostEstimate(flops=int(flops), bytes_accessed=int(moved), transcendentals=0)


def local(residual, attn_partial, norm_gain, expert_ids, route_scores, w_gate, w_down):
    bf16, f32 = jnp.bfloat16, jnp.float32
    tokens, share = residual.shape
    nt, ne = lax.axis_size("tensor"), lax.axis_size("expert")
    z, me = lax.axis_index("tensor"), lax.axis_index("expert")
    top = expert_ids.shape[1]
    cap = tokens * top // ne * 5 // 4
    rows = ne * cap
    ff = w_gate.shape[2] // nt
    me_arr = jnp.full((1,), me, jnp.int32)
    z_arr = jnp.full((1,), z, jnp.int32)
    sds = jax.ShapeDtypeStruct
    near, far = [0, 1], list(range(2, ne))

    def block(k):
        return lax.dynamic_slice(attn_partial[0], (0, k * share), (tokens, share))

    if nt == 4:
        end = (z == 0) | (z == 3)
        end_arr = jnp.where(end, 1, 0).astype(jnp.int32).reshape(1)
        relayed = exchange(block(jnp.where(end, z ^ 3, z ^ 1)), "tensor", 1)
        parts = [block(z)]
        parts.append(lax.ppermute(block(z ^ 3), "tensor", [(1, 2), (2, 1)]))
        parts.append(lax.ppermute(block(z ^ 2), "tensor", [(0, 2), (3, 1)]))
        merged = pl.pallas_call(
            merge_kernel,
            out_shape=sds((tokens, share), bf16),
            in_specs=[scalar()] + [whole()] * 3,
            out_specs=whole(),
            compiler_params=params(),
            cost_estimate=estimate(2 * tokens * share, 8 * tokens * share),
            name="merge",
        )(end_arr, block(z ^ 1), block(z ^ 2), relayed)
        parts.append(lax.ppermute(merged, "tensor", [(0, 1), (1, 3), (2, 0), (3, 2)]))
        parts.append(relayed)
    else:
        end_arr = jnp.ones((1,), jnp.int32)
        parts = [exchange(block(z ^ k), "tensor", k) if k else block(z) for k in partners(nt)]

    select, high, low = pl.pallas_call(
        functools.partial(routing_kernel, ne, cap),
        out_shape=(sds((rows, tokens), bf16), sds((tokens, rows), bf16), sds((tokens, rows), bf16)),
        in_specs=[scalar(), whole(), whole(), whole()],
        out_specs=(whole(),) * 3,
        compiler_params=params(),
        cost_estimate=estimate(10**6, 2**16),
        name="routing",
    )(me_arr, expert_ids, expert_ids.T, route_scores)

    fetched = (residual, w_gate)
    residual, w_gate = pl.pallas_call(
        fetch_kernel,
        out_shape=tuple(sds(v.shape, v.dtype) for v in fetched),
        in_specs=[anywhere()] * len(fetched),
        out_specs=(whole(),) * len(fetched),
        scratch_shapes=[pltpu.SemaphoreType.DMA((len(fetched),))],
        compiler_params=params(),
        cost_estimate=estimate(10**6, sum(2 * v.size for v in fetched)),
        name="fetch",
    )(*fetched)

    kept, *near_rows = pl.pallas_call(
        functools.partial(add_kernel, len(parts), cap, near),
        out_shape=(sds((tokens, share), bf16),) + (sds((cap, share), bf16),) * len(near),
        in_specs=[scalar()] + [whole()] * (2 + len(parts)),
        out_specs=(whole(),) * (1 + len(near)),
        compiler_params=params(),
        cost_estimate=estimate(2 * rows * tokens * share, 4 * tokens * share * nt),
        name="add",
    )(end_arr, residual, select, *parts)
    arrived = {0: near_rows[0], 1: exchange(near_rows[1], "expert", 1)}
    far_rows = pl.pallas_call(
        functools.partial(pack_kernel, cap, far),
        out_shape=(sds((cap, share), bf16),) * len(far),
        in_specs=[whole()] * 2,
        out_specs=(whole(),) * len(far),
        compiler_params=params(),
        cost_estimate=estimate(2 * rows * tokens * share, 4 * tokens * share),
        name="pack",
    )(kept, select)
    for k, value in zip(far, far_rows):
        arrived[k] = exchange(value, "expert", k)

    stored = []

    def summed_gate(ks, after=None):
        count = len(ks) * cap
        lhs, squares = pl.pallas_call(
            functools.partial(prepare_kernel, len(ks)),
            out_shape=(sds((count, share), bf16), sds((8, count), f32)),
            in_specs=[whole()] * (1 + len(ks)),
            out_specs=(whole(),) * 2,
            compiler_params=params(),
            cost_estimate=estimate(16 * count * share, 4 * count * share),
            name="prepare",
        )(norm_gain[None, :], *[arrived[k] for k in ks])
        tall = count + extra_rows(count, ff)
        gates = {}
        for k in partners(nt):
            earlier = [] if after is None else [after[k or 1]]
            if k == 0 and after is not None:
                stored.append(
                    pl.pallas_call(
                        store_kernel,
                        out_shape=sds((tokens, share), bf16),
                        in_specs=[whole(), anywhere()],
                        out_specs=whole(),
                        compiler_params=params(),
                        cost_estimate=estimate(10**6, 4 * tokens * share),
                        name="store",
                    )(kept, partial_gate)
                )
                earlier.append(stored[0])
            partial_gate = pl.pallas_call(
                gate_kernel,
                out_shape=sds((tall, ff), bf16),
                grid_spec=pltpu.PrefetchScalarGridSpec(
                    num_scalar_prefetch=1,
                    grid=(1,),
                    in_specs=[
                        pl.BlockSpec((count, share), lambda i, b: (0, 0)),
                        pl.BlockSpec((8, count), lambda i, b: (0, 0)),
                        pl.BlockSpec((1, share, ff), lambda i, b: (0, 0, b[0])),
                    ]
                    + [anywhere()] * len(earlier),
                    out_specs=pl.BlockSpec((tall, ff), lambda i, b: (0, 0)),
                ),
                compiler_params=params(),
                cost_estimate=estimate(2 * count * share * ff, 2 * share * ff),
                name="gate",
            )(z_arr ^ k, lhs, squares, w_gate, *earlier)
            gates[k] = exchange(partial_gate, "tensor", k) if k else partial_gate
        return gates

    def gathered_hidden(ks, gates, after=()):
        count = len(ks) * cap
        own = pl.pallas_call(
            functools.partial(activate_kernel, nt, count, float(share * nt)),
            out_shape=sds((count, ff), bf16),
            in_specs=[whole()] * nt + [anywhere()] * len(after),
            out_specs=whole(),
            compiler_params=params(),
            cost_estimate=estimate(20 * count * ff, 2 * count * ff * (nt + 1)),
            name="activate",
        )(*[gates[k] for k in range(nt)], *after)
        return {k: exchange(own, "tensor", k) if k else own for k in partners(nt)}

    def produced(ks, hidden):
        outs = pl.pallas_call(
            functools.partial(down_kernel, nt, len(ks), cap),
            out_shape=(sds((cap, share), bf16),) * len(ks),
            in_specs=[scalar(), whole()] + [whole()] * nt,
            out_specs=(whole(),) * len(ks),
            compiler_params=params(),
            cost_estimate=estimate(2 * len(ks) * cap * share * ff * nt, 2 * share * ff * nt),
            name="down",
        )(z_arr, w_down, *[hidden[k] for k in partners(nt)])
        return dict(zip(ks, outs))

    near_gates = summed_gate(near)
    far_gates = summed_gate(far, near_gates)
    far_hidden = gathered_hidden(far, far_gates)
    near_hidden = gathered_hidden(near, near_gates, (far_hidden[3],))
    returned = {}
    for ks, hidden in ((far, far_hidden), (near, near_hidden)):
        for k, value in produced(ks, hidden).items():
            returned[k] = exchange(value, "expert", k) if k else value

    moe_out = pl.pallas_call(
        functools.partial(combine_kernel, ne),
        out_shape=sds((tokens, share), bf16),
        in_specs=[whole()] * (2 + ne),
        out_specs=whole(),
        compiler_params=params(),
        cost_estimate=estimate(4 * rows * tokens * share, 2 * rows * share),
        name="combine",
    )(high, low, *[returned[k] for k in range(ne)])
    return stored[0], moe_out


def solution(mesh):
    return jax.shard_map(
        local,
        mesh=mesh,
        in_specs=(
            P(("groups", "expert"), "tensor"),
            P("tensor", ("groups", "expert"), None),
            P("tensor"),
            P(("groups", "expert"), None),
            P(("groups", "expert"), None),
            P("expert", "tensor", None),
            P("expert", None, "tensor"),
        ),
        out_specs=(P(("groups", "expert"), "tensor"), P(("groups", "expert"), "tensor")),
        check_vma=False,
    )
```

```python
import functools

import jax
import jax.numpy as jnp
from jax import lax
from jax.experimental import pallas as pl
from jax.experimental.pallas import tpu as pltpu
from jax.sharding import PartitionSpec as P


def partners(n):
    return list(range(n - 1, -1, -1))


def exchange(value, axis, step):
    n = lax.axis_size(axis)
    return lax.ppermute(value, axis, [(i, i ^ step) for i in range(n)])


def params(mib=16):
    return pltpu.CompilerParams(vmem_limit_bytes=mib << 20)


def whole():
    return pl.BlockSpec(memory_space=pltpu.VMEM)


def anywhere():
    return pl.BlockSpec(memory_space=pl.ANY)


def scalar():
    return pl.BlockSpec(memory_space=pltpu.SMEM)


def routing_kernel(n, cap, me_ref, ids_ref, idst_ref, scores_ref, select_ref, high_ref, low_ref):
    me = me_ref[0]
    tokens, top = ids_ref.shape
    f32, bf16 = jnp.float32, jnp.bfloat16
    row = lax.broadcasted_iota(jnp.int32, (tokens, tokens), 0)
    col = lax.broadcasted_iota(jnp.int32, (tokens, tokens), 1)
    before_t = jnp.where(row < col, 1.0, 0.0).astype(bf16)
    before = jnp.where(col < row, 1.0, 0.0).astype(bf16)
    scores = scores_ref[...]
    weights = 2.827 * scores / jnp.sum(scores, axis=1, keepdims=True)
    slot_t = lax.broadcasted_iota(jnp.int32, (cap, tokens), 0)
    slot = lax.broadcasted_iota(jnp.int32, (tokens, cap), 1)
    selects, highs, lows = [], [], []
    for k in range(n):
        expert = me ^ k
        named_t = jnp.zeros((1, tokens), f32)
        named = jnp.zeros((tokens, 1), f32)
        weight = jnp.zeros((tokens, 1), f32)
        for j in range(top):
            hit = jnp.where(ids_ref[:, j : j + 1] == expert, 1.0, 0.0)
            named_t += jnp.where(idst_ref[j : j + 1, :] == expert, 1.0, 0.0)
            named += hit
            weight += hit * weights[:, j : j + 1]
        place_t = jnp.dot(
            jnp.broadcast_to(named_t, (8, tokens)).astype(bf16), before_t, preferred_element_type=f32
        )[0:1, :].astype(jnp.int32)
        place = jnp.dot(
            before, jnp.broadcast_to(named, (tokens, 128)).astype(bf16), preferred_element_type=f32
        )[:, 0:1].astype(jnp.int32)
        selects.append(jnp.where(place_t == slot_t, jnp.broadcast_to(named_t, slot_t.shape), 0.0))
        full = jnp.where(place == slot, jnp.broadcast_to(weight, slot.shape), 0.0)
        high = full.astype(bf16).astype(f32)
        highs.append(high)
        lows.append(full - high)
    select_ref[...] = jnp.concatenate(selects, axis=0).astype(bf16)
    high_ref[...] = jnp.concatenate(highs, axis=1).astype(bf16)
    low_ref[...] = jnp.concatenate(lows, axis=1).astype(bf16)


def fetch_kernel(*refs):
    *pairs, sems = refs
    half = len(pairs) // 2
    copies = [pltpu.make_async_copy(pairs[i], pairs[half + i], sems.at[i]) for i in range(half)]
    for copy in copies:
        copy.start()
    for copy in copies:
        copy.wait()


def merge_kernel(end_ref, own_ref, passing_ref, relayed_ref, out_ref):
    @pl.when(end_ref[0] == 1)
    def _():
        out_ref[...] = own_ref[...]

    @pl.when(end_ref[0] == 0)
    def _():
        total = passing_ref[...].astype(jnp.float32) + relayed_ref[...].astype(jnp.float32)
        out_ref[...] = total.astype(jnp.bfloat16)


def add_kernel(n_tensor, cap, ks, last_ref, residual_ref, select_ref, *refs):
    parts, kept_ref, outs = refs[:n_tensor], refs[n_tensor], refs[n_tensor + 1 :]
    total = residual_ref[...].astype(jnp.float32)
    for part in parts[:-1]:
        total += part[...].astype(jnp.float32)
    total += jnp.where(last_ref[0] == 1, parts[-1][...].astype(jnp.float32), 0.0)
    kept_ref[...] = total.astype(jnp.bfloat16)
    pack_kernel(cap, ks, kept_ref, select_ref, *outs)


def pack_kernel(cap, ks, stream_ref, select_ref, *outs):
    first, last = ks[0] * cap, (ks[-1] + 1) * cap
    packed = jnp.dot(select_ref[first:last, :], stream_ref[...], preferred_element_type=jnp.float32)
    for i, out in enumerate(outs):
        out[...] = packed[i * cap : (i + 1) * cap, :].astype(jnp.bfloat16)


def store_kernel(values_ref, after_ref, out_ref):
    out_ref[...] = values_ref[...]


def prepare_kernel(n, gain_ref, *refs):
    pieces, lhs_ref, squares_ref = refs[:n], refs[-2], refs[-1]
    rows = jnp.concatenate([p[...].astype(jnp.float32) for p in pieces], axis=0)
    squared = (rows * rows).astype(jnp.bfloat16)
    ones = jnp.ones((8, rows.shape[1]), jnp.bfloat16)
    sums = lax.dot_general(ones, squared, (((1,), (1,)), ((), ())), preferred_element_type=jnp.float32)
    high = sums.astype(jnp.bfloat16).astype(jnp.float32)
    low = sums - high
    which = lax.broadcasted_iota(jnp.int32, sums.shape, 0)
    squares_ref[...] = jnp.where(which == 0, high, jnp.where(which == 1, low, 0.0))
    lhs_ref[...] = (rows * gain_ref[...].astype(jnp.float32)).astype(jnp.bfloat16)


def extra_rows(rows, width):
    return -(-2 * -(-rows // width) // 8) * 8


def gate_kernel(block_ref, lhs_ref, squares_ref, w_ref, *refs):
    out_ref = refs[-1]
    rows = lhs_ref.shape[0]
    width = out_ref.shape[1]
    extra = extra_rows(rows, width)
    product = jnp.dot(lhs_ref[...], w_ref[0], preferred_element_type=jnp.float32)
    squares = squares_ref[...]
    pieces = -(-rows // width)
    if rows % width:
        squares = jnp.concatenate([squares, jnp.zeros((8, width - rows % width), jnp.float32)], axis=1)
    if pieces == 1:
        below = squares
    else:
        below = jnp.concatenate(
            [squares[0:2, i * width : (i + 1) * width] for i in range(pieces)]
            + ([jnp.zeros((extra - 2 * pieces, width), jnp.float32)] if extra > 2 * pieces else []),
            axis=0,
        )
    out_ref[...] = jnp.concatenate([product, below], axis=0).astype(jnp.bfloat16)


def activate_kernel(n, rows, features, *refs):
    parts, out_ref = refs[:n], refs[-1]
    f32, bf16 = jnp.float32, jnp.bfloat16
    width = out_ref.shape[1]
    total, squares = None, None
    for part in parts:
        value = part[...].astype(f32)
        gate = value[:rows]
        extra = value[rows:]
        total = gate if total is None else total + gate
        squares = extra if squares is None else squares + extra
    pieces = -(-rows // width)
    lines = [squares[2 * i : 2 * i + 1] + squares[2 * i + 1 : 2 * i + 2] for i in range(pieces)]
    line = (lines[0] if pieces == 1 else jnp.concatenate(lines, axis=1))[:, :rows]
    inverse = lax.rsqrt(line / features + 1e-06)
    column = jnp.transpose(jnp.broadcast_to(inverse, (8, rows)))[:, 0:1]
    gate = total * column
    out_ref[...] = (gate / (1.0 + jnp.exp(-gate))).astype(bf16)


def down_kernel(n_tensor, n, cap, block_ref, w_ref, *refs):
    pieces, outs = refs[:n_tensor], refs[n_tensor:]
    width = pieces[0].shape[1]
    total = None
    for i, k in enumerate(partners(n_tensor)):
        start = pl.multiple_of((block_ref[0] ^ k) * width, width)
        term = jnp.dot(pieces[i][...], w_ref[0, pl.ds(start, width), :], preferred_element_type=jnp.float32)
        total = term if total is None else total + term
    for k in range(n):
        outs[k][...] = total[k * cap : (k + 1) * cap, :].astype(jnp.bfloat16)


def combine_kernel(n, high_ref, low_ref, *refs):
    pieces, out_ref = refs[:n], refs[n]
    rows = jnp.concatenate([p[...].astype(jnp.float32) for p in pieces], axis=0).astype(jnp.bfloat16)
    total = jnp.dot(high_ref[...], rows, preferred_element_type=jnp.float32)
    total += jnp.dot(low_ref[...], rows, preferred_element_type=jnp.float32)
    out_ref[...] = total.astype(jnp.bfloat16)


def estimate(flops, moved):
    return pl.CostEstimate(flops=int(flops), bytes_accessed=int(moved), transcendentals=0)


def local(residual, attn_partial, norm_gain, expert_ids, route_scores, w_gate, w_down):
    bf16, f32 = jnp.bfloat16, jnp.float32
    tokens, share = residual.shape
    nt, ne = lax.axis_size("tensor"), lax.axis_size("expert")
    z, me = lax.axis_index("tensor"), lax.axis_index("expert")
    top = expert_ids.shape[1]
    cap = tokens * top // ne * 5 // 4
    rows = ne * cap
    ff = w_gate.shape[2] // nt
    me_arr = jnp.full((1,), me, jnp.int32)
    z_arr = jnp.full((1,), z, jnp.int32)
    sds = jax.ShapeDtypeStruct
    near, far = [0, 1], list(range(2, ne))

    def block(k):
        return lax.dynamic_slice(attn_partial[0], (0, k * share), (tokens, share))

    if nt == 4:
        end = (z == 0) | (z == 3)
        end_arr = jnp.where(end, 1, 0).astype(jnp.int32).reshape(1)
        relayed = exchange(block(jnp.where(end, z ^ 3, z ^ 1)), "tensor", 1)
        parts = [block(z)]
        parts.append(lax.ppermute(block(z ^ 3), "tensor", [(1, 2), (2, 1)]))
        parts.append(lax.ppermute(block(z ^ 2), "tensor", [(0, 2), (3, 1)]))
        merged = pl.pallas_call(
            merge_kernel,
            out_shape=sds((tokens, share), bf16),
            in_specs=[scalar()] + [whole()] * 3,
            out_specs=whole(),
            compiler_params=params(),
            cost_estimate=estimate(2 * tokens * share, 8 * tokens * share),
            name="merge",
        )(end_arr, block(z ^ 1), block(z ^ 2), relayed)
        parts.append(lax.ppermute(merged, "tensor", [(0, 1), (1, 3), (2, 0), (3, 2)]))
        parts.append(relayed)
    else:
        end_arr = jnp.ones((1,), jnp.int32)
        parts = [exchange(block(z ^ k), "tensor", k) if k else block(z) for k in partners(nt)]

    select, high, low = pl.pallas_call(
        functools.partial(routing_kernel, ne, cap),
        out_shape=(sds((rows, tokens), bf16), sds((tokens, rows), bf16), sds((tokens, rows), bf16)),
        in_specs=[scalar(), whole(), whole(), whole()],
        out_specs=(whole(),) * 3,
        compiler_params=params(),
        cost_estimate=estimate(10**6, 2**16),
        name="routing",
    )(me_arr, expert_ids, expert_ids.T, route_scores)

    fetched = (residual, w_gate)
    residual, w_gate = pl.pallas_call(
        fetch_kernel,
        out_shape=tuple(sds(v.shape, v.dtype) for v in fetched),
        in_specs=[anywhere()] * len(fetched),
        out_specs=(whole(),) * len(fetched),
        scratch_shapes=[pltpu.SemaphoreType.DMA((len(fetched),))],
        compiler_params=params(),
        cost_estimate=estimate(10**6, sum(2 * v.size for v in fetched)),
        name="fetch",
    )(*fetched)

    kept, *near_rows = pl.pallas_call(
        functools.partial(add_kernel, len(parts), cap, near),
        out_shape=(sds((tokens, share), bf16),) + (sds((cap, share), bf16),) * len(near),
        in_specs=[scalar()] + [whole()] * (2 + len(parts)),
        out_specs=(whole(),) * (1 + len(near)),
        compiler_params=params(),
        cost_estimate=estimate(2 * rows * tokens * share, 4 * tokens * share * nt),
        name="add",
    )(end_arr, residual, select, *parts)
    arrived = {0: near_rows[0], 1: exchange(near_rows[1], "expert", 1)}
    far_rows = pl.pallas_call(
        functools.partial(pack_kernel, cap, far),
        out_shape=(sds((cap, share), bf16),) * len(far),
        in_specs=[whole()] * 2,
        out_specs=(whole(),) * len(far),
        compiler_params=params(),
        cost_estimate=estimate(2 * rows * tokens * share, 4 * tokens * share),
        name="pack",
    )(kept, select)
    for k, value in zip(far, far_rows):
        arrived[k] = exchange(value, "expert", k)

    stored = []

    def summed_gate(ks, after=None):
        count = len(ks) * cap
        lhs, squares = pl.pallas_call(
            functools.partial(prepare_kernel, len(ks)),
            out_shape=(sds((count, share), bf16), sds((8, count), f32)),
            in_specs=[whole()] * (1 + len(ks)),
            out_specs=(whole(),) * 2,
            compiler_params=params(),
            cost_estimate=estimate(16 * count * share, 4 * count * share),
            name="prepare",
        )(norm_gain[None, :], *[arrived[k] for k in ks])
        tall = count + extra_rows(count, ff)
        gates = {}
        for k in ([1, 3, 2, 0] if nt == 4 and after is not None else partners(nt)):
            earlier = [] if after is None else [after[k or 1]]
            if k == 0 and after is not None:
                stored.append(
                    pl.pallas_call(
                        store_kernel,
                        out_shape=sds((tokens, share), bf16),
                        in_specs=[whole(), anywhere()],
                        out_specs=whole(),
                        compiler_params=params(),
                        cost_estimate=estimate(10**6, 4 * tokens * share),
                        name="store",
                    )(kept, partial_gate)
                )
                earlier.append(stored[0])
            partial_gate = pl.pallas_call(
                gate_kernel,
                out_shape=sds((tall, ff), bf16),
                grid_spec=pltpu.PrefetchScalarGridSpec(
                    num_scalar_prefetch=1,
                    grid=(1,),
                    in_specs=[
                        pl.BlockSpec((count, share), lambda i, b: (0, 0)),
                        pl.BlockSpec((8, count), lambda i, b: (0, 0)),
                        pl.BlockSpec((1, share, ff), lambda i, b: (0, 0, b[0])),
                    ]
                    + [anywhere()] * len(earlier),
                    out_specs=pl.BlockSpec((tall, ff), lambda i, b: (0, 0)),
                ),
                compiler_params=params(),
                cost_estimate=estimate(2 * count * share * ff, 2 * share * ff),
                name="gate",
            )(z_arr ^ k, lhs, squares, w_gate, *earlier)
            gates[k] = exchange(partial_gate, "tensor", k) if k else partial_gate
        return gates

    def gathered_hidden(ks, gates, after=()):
        count = len(ks) * cap
        own = pl.pallas_call(
            functools.partial(activate_kernel, nt, count, float(share * nt)),
            out_shape=sds((count, ff), bf16),
            in_specs=[whole()] * nt + [anywhere()] * len(after),
            out_specs=whole(),
            compiler_params=params(),
            cost_estimate=estimate(20 * count * ff, 2 * count * ff * (nt + 1)),
            name="activate",
        )(*[gates[k] for k in range(nt)], *after)
        return {k: exchange(own, "tensor", k) if k else own for k in partners(nt)}

    def produced(ks, hidden):
        outs = pl.pallas_call(
            functools.partial(down_kernel, nt, len(ks), cap),
            out_shape=(sds((cap, share), bf16),) * len(ks),
            in_specs=[scalar(), whole()] + [whole()] * nt,
            out_specs=(whole(),) * len(ks),
            compiler_params=params(),
            cost_estimate=estimate(2 * len(ks) * cap * share * ff * nt, 2 * share * ff * nt),
            name="down",
        )(z_arr, w_down, *[hidden[k] for k in partners(nt)])
        return dict(zip(ks, outs))

    near_gates = summed_gate(near)
    far_gates = summed_gate(far, near_gates)
    far_hidden = gathered_hidden(far, far_gates)
    near_hidden = gathered_hidden(near, near_gates, (far_hidden[3],))
    returned = {}
    for ks, hidden in ((far, far_hidden), (near, near_hidden)):
        for k, value in produced(ks, hidden).items():
            returned[k] = exchange(value, "expert", k) if k else value

    moe_out = pl.pallas_call(
        functools.partial(combine_kernel, ne),
        out_shape=sds((tokens, share), bf16),
        in_specs=[whole()] * (2 + ne),
        out_specs=whole(),
        compiler_params=params(),
        cost_estimate=estimate(4 * rows * tokens * share, 2 * rows * share),
        name="combine",
    )(high, low, *[returned[k] for k in range(ne)])
    return stored[0], moe_out


def solution(mesh):
    return jax.shard_map(
        local,
        mesh=mesh,
        in_specs=(
            P(("groups", "expert"), "tensor"),
            P("tensor", ("groups", "expert"), None),
            P("tensor"),
            P(("groups", "expert"), None),
            P(("groups", "expert"), None),
            P("expert", "tensor", None),
            P("expert", None, "tensor"),
        ),
        out_specs=(P(("groups", "expert"), "tensor"), P(("groups", "expert"), "tensor")),
        check_vma=False,
    )
```

```python
import functools

import jax
import jax.numpy as jnp
from jax import lax
from jax.experimental import pallas as pl
from jax.experimental.pallas import tpu as pltpu
from jax.sharding import PartitionSpec as P


def partners(n):
    return list(range(n - 1, -1, -1))


def exchange(value, axis, step):
    n = lax.axis_size(axis)
    return lax.ppermute(value, axis, [(i, i ^ step) for i in range(n)])


def params(mib=16):
    return pltpu.CompilerParams(vmem_limit_bytes=mib << 20)


def whole():
    return pl.BlockSpec(memory_space=pltpu.VMEM)


def anywhere():
    return pl.BlockSpec(memory_space=pl.ANY)


def scalar():
    return pl.BlockSpec(memory_space=pltpu.SMEM)


def routing_kernel(n, cap, me_ref, ids_ref, idst_ref, scores_ref, select_ref, high_ref, low_ref):
    me = me_ref[0]
    tokens, top = ids_ref.shape
    f32, bf16 = jnp.float32, jnp.bfloat16
    row = lax.broadcasted_iota(jnp.int32, (tokens, tokens), 0)
    col = lax.broadcasted_iota(jnp.int32, (tokens, tokens), 1)
    before_t = jnp.where(row < col, 1.0, 0.0).astype(bf16)
    before = jnp.where(col < row, 1.0, 0.0).astype(bf16)
    scores = scores_ref[...]
    weights = 2.827 * scores / jnp.sum(scores, axis=1, keepdims=True)
    slot_t = lax.broadcasted_iota(jnp.int32, (cap, tokens), 0)
    slot = lax.broadcasted_iota(jnp.int32, (tokens, cap), 1)
    selects, highs, lows = [], [], []
    for k in range(n):
        expert = me ^ k
        named_t = jnp.zeros((1, tokens), f32)
        named = jnp.zeros((tokens, 1), f32)
        weight = jnp.zeros((tokens, 1), f32)
        for j in range(top):
            hit = jnp.where(ids_ref[:, j : j + 1] == expert, 1.0, 0.0)
            named_t += jnp.where(idst_ref[j : j + 1, :] == expert, 1.0, 0.0)
            named += hit
            weight += hit * weights[:, j : j + 1]
        place_t = jnp.dot(
            jnp.broadcast_to(named_t, (8, tokens)).astype(bf16), before_t, preferred_element_type=f32
        )[0:1, :].astype(jnp.int32)
        place = jnp.dot(
            before, jnp.broadcast_to(named, (tokens, 128)).astype(bf16), preferred_element_type=f32
        )[:, 0:1].astype(jnp.int32)
        selects.append(jnp.where(place_t == slot_t, jnp.broadcast_to(named_t, slot_t.shape), 0.0))
        full = jnp.where(place == slot, jnp.broadcast_to(weight, slot.shape), 0.0)
        high = full.astype(bf16).astype(f32)
        highs.append(high)
        lows.append(full - high)
    select_ref[...] = jnp.concatenate(selects, axis=0).astype(bf16)
    high_ref[...] = jnp.concatenate(highs, axis=1).astype(bf16)
    low_ref[...] = jnp.concatenate(lows, axis=1).astype(bf16)


def fetch_kernel(*refs):
    *pairs, sems = refs
    half = len(pairs) // 2
    copies = [pltpu.make_async_copy(pairs[i], pairs[half + i], sems.at[i]) for i in range(half)]
    for copy in copies:
        copy.start()
    for copy in copies:
        copy.wait()


def merge_kernel(end_ref, own_ref, passing_ref, relayed_ref, out_ref):
    @pl.when(end_ref[0] == 1)
    def _():
        out_ref[...] = own_ref[...]

    @pl.when(end_ref[0] == 0)
    def _():
        total = passing_ref[...].astype(jnp.float32) + relayed_ref[...].astype(jnp.float32)
        out_ref[...] = total.astype(jnp.bfloat16)


def add_kernel(n_tensor, cap, ks, last_ref, residual_ref, select_ref, *refs):
    parts, kept_ref, outs = refs[:n_tensor], refs[n_tensor], refs[n_tensor + 1 :]
    total = residual_ref[...].astype(jnp.float32)
    for part in parts[:-1]:
        total += part[...].astype(jnp.float32)
    total += jnp.where(last_ref[0] == 1, parts[-1][...].astype(jnp.float32), 0.0)
    kept_ref[...] = total.astype(jnp.bfloat16)
    pack_kernel(cap, ks, kept_ref, select_ref, *outs)


def pack_kernel(cap, ks, stream_ref, select_ref, *outs):
    first, last = ks[0] * cap, (ks[-1] + 1) * cap
    packed = jnp.dot(select_ref[first:last, :], stream_ref[...], preferred_element_type=jnp.float32)
    for i, out in enumerate(outs):
        out[...] = packed[i * cap : (i + 1) * cap, :].astype(jnp.bfloat16)


def hold_kernel(value_ref, *refs):
    refs[-1][...] = value_ref[...]


def store_kernel(values_ref, after_ref, out_ref, token_ref):
    out_ref[...] = values_ref[...]
    token_ref[...] = jnp.zeros(token_ref.shape, token_ref.dtype)


def prepare_kernel(n, gain_ref, *refs):
    pieces, lhs_ref, squares_ref = refs[:n], refs[-2], refs[-1]
    rows = jnp.concatenate([p[...].astype(jnp.float32) for p in pieces], axis=0)
    squared = (rows * rows).astype(jnp.bfloat16)
    ones = jnp.ones((8, rows.shape[1]), jnp.bfloat16)
    sums = lax.dot_general(ones, squared, (((1,), (1,)), ((), ())), preferred_element_type=jnp.float32)
    high = sums.astype(jnp.bfloat16).astype(jnp.float32)
    low = sums - high
    which = lax.broadcasted_iota(jnp.int32, sums.shape, 0)
    squares_ref[...] = jnp.where(which == 0, high, jnp.where(which == 1, low, 0.0))
    lhs_ref[...] = (rows * gain_ref[...].astype(jnp.float32)).astype(jnp.bfloat16)


def extra_rows(rows, width):
    return -(-2 * -(-rows // width) // 8) * 8


def gate_kernel(block_ref, lhs_ref, squares_ref, w_ref, *refs):
    out_ref = refs[-1]
    rows = lhs_ref.shape[0]
    width = out_ref.shape[1]
    extra = extra_rows(rows, width)
    product = jnp.dot(lhs_ref[...], w_ref[0], preferred_element_type=jnp.float32)
    squares = squares_ref[...]
    pieces = -(-rows // width)
    if rows % width:
        squares = jnp.concatenate([squares, jnp.zeros((8, width - rows % width), jnp.float32)], axis=1)
    if pieces == 1:
        below = squares
    else:
        below = jnp.concatenate(
            [squares[0:2, i * width : (i + 1) * width] for i in range(pieces)]
            + ([jnp.zeros((extra - 2 * pieces, width), jnp.float32)] if extra > 2 * pieces else []),
            axis=0,
        )
    out_ref[...] = jnp.concatenate([product, below], axis=0).astype(jnp.bfloat16)


def activate_kernel(n, rows, features, *refs):
    parts, out_ref = refs[:n], refs[-1]
    f32, bf16 = jnp.float32, jnp.bfloat16
    width = out_ref.shape[1]
    total, squares = None, None
    for part in parts:
        value = part[...].astype(f32)
        gate = value[:rows]
        extra = value[rows:]
        total = gate if total is None else total + gate
        squares = extra if squares is None else squares + extra
    pieces = -(-rows // width)
    lines = [squares[2 * i : 2 * i + 1] + squares[2 * i + 1 : 2 * i + 2] for i in range(pieces)]
    line = (lines[0] if pieces == 1 else jnp.concatenate(lines, axis=1))[:, :rows]
    inverse = lax.rsqrt(line / features + 1e-06)
    column = jnp.transpose(jnp.broadcast_to(inverse, (8, rows)))[:, 0:1]
    gate = total * column
    out_ref[...] = (gate / (1.0 + jnp.exp(-gate))).astype(bf16)


def down_kernel(n_tensor, n, cap, block_ref, w_ref, *refs):
    pieces, outs = refs[:n_tensor], refs[n_tensor:]
    width = pieces[0].shape[1]
    total = None
    for i, k in enumerate(partners(n_tensor)):
        start = pl.multiple_of((block_ref[0] ^ k) * width, width)
        term = jnp.dot(pieces[i][...], w_ref[0, pl.ds(start, width), :], preferred_element_type=jnp.float32)
        total = term if total is None else total + term
    for k in range(n):
        outs[k][...] = total[k * cap : (k + 1) * cap, :].astype(jnp.bfloat16)


def combine_kernel(n, high_ref, low_ref, *refs):
    pieces, out_ref = refs[:n], refs[n]
    rows = jnp.concatenate([p[...].astype(jnp.float32) for p in pieces], axis=0).astype(jnp.bfloat16)
    total = jnp.dot(high_ref[...], rows, preferred_element_type=jnp.float32)
    total += jnp.dot(low_ref[...], rows, preferred_element_type=jnp.float32)
    out_ref[...] = total.astype(jnp.bfloat16)


def estimate(flops, moved):
    return pl.CostEstimate(flops=int(flops), bytes_accessed=int(moved), transcendentals=0)


def local(residual, attn_partial, norm_gain, expert_ids, route_scores, w_gate, w_down):
    bf16, f32 = jnp.bfloat16, jnp.float32
    tokens, share = residual.shape
    nt, ne = lax.axis_size("tensor"), lax.axis_size("expert")
    z, me = lax.axis_index("tensor"), lax.axis_index("expert")
    top = expert_ids.shape[1]
    cap = tokens * top // ne * 5 // 4
    rows = ne * cap
    ff = w_gate.shape[2] // nt
    me_arr = jnp.full((1,), me, jnp.int32)
    z_arr = jnp.full((1,), z, jnp.int32)
    sds = jax.ShapeDtypeStruct
    near, far = [0, 1], list(range(2, ne))

    def block(k):
        return lax.dynamic_slice(attn_partial[0], (0, k * share), (tokens, share))

    if nt == 4:
        end = (z == 0) | (z == 3)
        end_arr = jnp.where(end, 1, 0).astype(jnp.int32).reshape(1)
        relayed = exchange(block(jnp.where(end, z ^ 3, z ^ 1)), "tensor", 1)
        parts = [block(z)]
        parts.append(lax.ppermute(block(z ^ 3), "tensor", [(1, 2), (2, 1)]))
        parts.append(lax.ppermute(block(z ^ 2), "tensor", [(0, 2), (3, 1)]))
        merged = pl.pallas_call(
            merge_kernel,
            out_shape=sds((tokens, share), bf16),
            in_specs=[scalar()] + [whole()] * 3,
            out_specs=whole(),
            compiler_params=params(),
            cost_estimate=estimate(2 * tokens * share, 8 * tokens * share),
            name="merge",
        )(end_arr, block(z ^ 1), block(z ^ 2), relayed)
        parts.append(lax.ppermute(merged, "tensor", [(0, 1), (1, 3), (2, 0), (3, 2)]))
        parts.append(relayed)
    else:
        end_arr = jnp.ones((1,), jnp.int32)
        parts = [exchange(block(z ^ k), "tensor", k) if k else block(z) for k in partners(nt)]

    select, high, low = pl.pallas_call(
        functools.partial(routing_kernel, ne, cap),
        out_shape=(sds((rows, tokens), bf16), sds((tokens, rows), bf16), sds((tokens, rows), bf16)),
        in_specs=[scalar(), whole(), whole(), whole()],
        out_specs=(whole(),) * 3,
        compiler_params=params(),
        cost_estimate=estimate(10**6, 2**16),
        name="routing",
    )(me_arr, expert_ids, expert_ids.T, route_scores)

    fetched = (residual, w_gate)
    residual, w_gate = pl.pallas_call(
        fetch_kernel,
        out_shape=tuple(sds(v.shape, v.dtype) for v in fetched),
        in_specs=[anywhere()] * len(fetched),
        out_specs=(whole(),) * len(fetched),
        scratch_shapes=[pltpu.SemaphoreType.DMA((len(fetched),))],
        compiler_params=params(),
        cost_estimate=estimate(10**6, sum(2 * v.size for v in fetched)),
        name="fetch",
    )(*fetched)

    kept, *near_rows = pl.pallas_call(
        functools.partial(add_kernel, len(parts), cap, near),
        out_shape=(sds((tokens, share), bf16),) + (sds((cap, share), bf16),) * len(near),
        in_specs=[scalar()] + [whole()] * (2 + len(parts)),
        out_specs=(whole(),) * (1 + len(near)),
        compiler_params=params(),
        cost_estimate=estimate(2 * rows * tokens * share, 4 * tokens * share * nt),
        name="add",
    )(end_arr, residual, select, *parts)
    arrived = {0: near_rows[0], 1: exchange(near_rows[1], "expert", 1)}
    far_rows = pl.pallas_call(
        functools.partial(pack_kernel, cap, far),
        out_shape=(sds((cap, share), bf16),) * len(far),
        in_specs=[whole()] * 2,
        out_specs=(whole(),) * len(far),
        compiler_params=params(),
        cost_estimate=estimate(2 * rows * tokens * share, 4 * tokens * share),
        name="pack",
    )(kept, select)
    for k, value in zip(far, far_rows):
        arrived[k] = exchange(value, "expert", k)

    stored = []

    def summed_gate(ks, after=None):
        count = len(ks) * cap
        lhs, squares = pl.pallas_call(
            functools.partial(prepare_kernel, len(ks)),
            out_shape=(sds((count, share), bf16), sds((8, count), f32)),
            in_specs=[whole()] * (1 + len(ks)),
            out_specs=(whole(),) * 2,
            compiler_params=params(),
            cost_estimate=estimate(16 * count * share, 4 * count * share),
            name="prepare",
        )(norm_gain[None, :], *[arrived[k] for k in ks])
        tall = count + extra_rows(count, ff)
        gates = {}
        for k in ([1, 3, 2, 0] if nt == 4 and after is not None else partners(nt)):
            earlier = [] if after is None else [after[k or 1]]
            if k == 0 and after is not None:
                written, token = pl.pallas_call(
                    store_kernel,
                    out_shape=(sds((tokens, share), bf16), sds((8, 128), f32)),
                    in_specs=[whole(), anywhere()],
                    out_specs=(whole(), whole()),
                    compiler_params=params(),
                    cost_estimate=estimate(10**6, 4 * tokens * share),
                    name="store",
                )(kept, partial_gate)
                stored.append(written)
                earlier.append(token)
            partial_gate = pl.pallas_call(
                gate_kernel,
                out_shape=sds((tall, ff), bf16),
                grid_spec=pltpu.PrefetchScalarGridSpec(
                    num_scalar_prefetch=1,
                    grid=(1,),
                    in_specs=[
                        pl.BlockSpec((count, share), lambda i, b: (0, 0)),
                        pl.BlockSpec((8, count), lambda i, b: (0, 0)),
                        pl.BlockSpec((1, share, ff), lambda i, b: (0, 0, b[0])),
                    ]
                    + [anywhere()] * len(earlier),
                    out_specs=pl.BlockSpec((tall, ff), lambda i, b: (0, 0)),
                ),
                compiler_params=params(),
                cost_estimate=estimate(2 * count * share * ff, 2 * share * ff),
                name="gate",
            )(z_arr ^ k, lhs, squares, w_gate, *earlier)
            gates[k] = exchange(partial_gate, "tensor", k) if k else partial_gate
        return gates

    def activated(ks, gates, after=()):
        count = len(ks) * cap
        return pl.pallas_call(
            functools.partial(activate_kernel, nt, count, float(share * nt)),
            out_shape=sds((count, ff), bf16),
            in_specs=[whole()] * nt + [anywhere()] * len(after),
            out_specs=whole(),
            compiler_params=params(),
            cost_estimate=estimate(20 * count * ff, 2 * count * ff * (nt + 1)),
            name="activate",
        )(*[gates[k] for k in range(nt)], *after)

    def held(value, *after):
        return pl.pallas_call(
            hold_kernel,
            out_shape=sds(value.shape, value.dtype),
            in_specs=[whole()] + [anywhere()] * len(after),
            out_specs=whole(),
            compiler_params=params(),
            cost_estimate=estimate(10**6, 4 * value.size),
            name="hold",
        )(value, *after)

    def produced(ks, hidden):
        outs = pl.pallas_call(
            functools.partial(down_kernel, nt, len(ks), cap),
            out_shape=(sds((cap, share), bf16),) * len(ks),
            in_specs=[scalar(), whole()] + [whole()] * nt,
            out_specs=(whole(),) * len(ks),
            compiler_params=params(),
            cost_estimate=estimate(2 * len(ks) * cap * share * ff * nt, 2 * share * ff * nt),
            name="down",
        )(z_arr, w_down, *[hidden[k] for k in partners(nt)])
        return dict(zip(ks, outs))

    near_gates = summed_gate(near)
    far_gates = summed_gate(far, near_gates)
    near_own = activated(near, near_gates)
    near_hidden = {0: near_own, 1: exchange(near_own, "tensor", 1)}
    far_own = activated(far, far_gates, (near_own,))
    far_hidden = {k: exchange(far_own, "tensor", k) if k else far_own for k in partners(nt)}
    waiting = held(near_own, far_hidden[3], near_hidden[1])
    near_hidden.update({k: exchange(waiting, "tensor", k) for k in partners(nt) if k > 1})
    returned = {}
    for ks, hidden in ((far, far_hidden), (near, near_hidden)):
        for k, value in produced(ks, hidden).items():
            returned[k] = exchange(value, "expert", k) if k else value

    moe_out = pl.pallas_call(
        functools.partial(combine_kernel, ne),
        out_shape=sds((tokens, share), bf16),
        in_specs=[whole()] * (2 + ne),
        out_specs=whole(),
        compiler_params=params(),
        cost_estimate=estimate(4 * rows * tokens * share, 2 * rows * share),
        name="combine",
    )(high, low, *[returned[k] for k in range(ne)])
    return stored[0], moe_out


def solution(mesh):
    return jax.shard_map(
        local,
        mesh=mesh,
        in_specs=(
            P(("groups", "expert"), "tensor"),
            P("tensor", ("groups", "expert"), None),
            P("tensor"),
            P(("groups", "expert"), None),
            P(("groups", "expert"), None),
            P("expert", "tensor", None),
            P("expert", None, "tensor"),
        ),
        out_specs=(P(("groups", "expert"), "tensor"), P(("groups", "expert"), "tensor")),
        check_vma=False,
    )
```

```python
import functools

import jax
import jax.numpy as jnp
from jax import lax
from jax.experimental import pallas as pl
from jax.experimental.pallas import tpu as pltpu
from jax.sharding import PartitionSpec as P


def partners(n):
    return list(range(n - 1, -1, -1))


def exchange(value, axis, step):
    n = lax.axis_size(axis)
    return lax.ppermute(value, axis, [(i, i ^ step) for i in range(n)])


def params(mib=16):
    return pltpu.CompilerParams(vmem_limit_bytes=mib << 20)


def whole():
    return pl.BlockSpec(memory_space=pltpu.VMEM)


def anywhere():
    return pl.BlockSpec(memory_space=pl.ANY)


def scalar():
    return pl.BlockSpec(memory_space=pltpu.SMEM)


def routing_kernel(n, cap, me_ref, ids_ref, idst_ref, scores_ref, select_ref, high_ref, low_ref):
    me = me_ref[0]
    tokens, top = ids_ref.shape
    f32, bf16 = jnp.float32, jnp.bfloat16
    row = lax.broadcasted_iota(jnp.int32, (tokens, tokens), 0)
    col = lax.broadcasted_iota(jnp.int32, (tokens, tokens), 1)
    before_t = jnp.where(row < col, 1.0, 0.0).astype(bf16)
    before = jnp.where(col < row, 1.0, 0.0).astype(bf16)
    scores = scores_ref[...]
    weights = 2.827 * scores / jnp.sum(scores, axis=1, keepdims=True)
    slot_t = lax.broadcasted_iota(jnp.int32, (cap, tokens), 0)
    slot = lax.broadcasted_iota(jnp.int32, (tokens, cap), 1)
    selects, highs, lows = [], [], []
    for k in range(n):
        expert = me ^ k
        named_t = jnp.zeros((1, tokens), f32)
        named = jnp.zeros((tokens, 1), f32)
        weight = jnp.zeros((tokens, 1), f32)
        for j in range(top):
            hit = jnp.where(ids_ref[:, j : j + 1] == expert, 1.0, 0.0)
            named_t += jnp.where(idst_ref[j : j + 1, :] == expert, 1.0, 0.0)
            named += hit
            weight += hit * weights[:, j : j + 1]
        place_t = jnp.dot(
            jnp.broadcast_to(named_t, (8, tokens)).astype(bf16), before_t, preferred_element_type=f32
        )[0:1, :].astype(jnp.int32)
        place = jnp.dot(
            before, jnp.broadcast_to(named, (tokens, 128)).astype(bf16), preferred_element_type=f32
        )[:, 0:1].astype(jnp.int32)
        selects.append(jnp.where(place_t == slot_t, jnp.broadcast_to(named_t, slot_t.shape), 0.0))
        full = jnp.where(place == slot, jnp.broadcast_to(weight, slot.shape), 0.0)
        high = full.astype(bf16).astype(f32)
        highs.append(high)
        lows.append(full - high)
    select_ref[...] = jnp.concatenate(selects, axis=0).astype(bf16)
    high_ref[...] = jnp.concatenate(highs, axis=1).astype(bf16)
    low_ref[...] = jnp.concatenate(lows, axis=1).astype(bf16)


def fetch_kernel(*refs):
    *pairs, sems = refs
    half = len(pairs) // 2
    copies = [pltpu.make_async_copy(pairs[i], pairs[half + i], sems.at[i]) for i in range(half)]
    for copy in copies:
        copy.start()
    for copy in copies:
        copy.wait()


def merge_kernel(end_ref, own_ref, passing_ref, relayed_ref, out_ref):
    @pl.when(end_ref[0] == 1)
    def _():
        out_ref[...] = own_ref[...]

    @pl.when(end_ref[0] == 0)
    def _():
        total = passing_ref[...].astype(jnp.float32) + relayed_ref[...].astype(jnp.float32)
        out_ref[...] = total.astype(jnp.bfloat16)


def add_kernel(n_tensor, cap, ks, last_ref, residual_ref, select_ref, *refs):
    parts, kept_ref, outs = refs[:n_tensor], refs[n_tensor], refs[n_tensor + 1 :]
    total = residual_ref[...].astype(jnp.float32)
    for part in parts[:-1]:
        total += part[...].astype(jnp.float32)
    total += jnp.where(last_ref[0] == 1, parts[-1][...].astype(jnp.float32), 0.0)
    kept_ref[...] = total.astype(jnp.bfloat16)
    pack_kernel(cap, ks, kept_ref, select_ref, *outs)


def pack_kernel(cap, ks, stream_ref, select_ref, *outs):
    first, last = ks[0] * cap, (ks[-1] + 1) * cap
    packed = jnp.dot(select_ref[first:last, :], stream_ref[...], preferred_element_type=jnp.float32)
    for i, out in enumerate(outs):
        out[...] = packed[i * cap : (i + 1) * cap, :].astype(jnp.bfloat16)


def hold_kernel(value_ref, *refs):
    refs[-1][...] = value_ref[...]


def store_kernel(values_ref, after_ref, out_ref, token_ref):
    out_ref[...] = values_ref[...]
    token_ref[...] = jnp.zeros(token_ref.shape, token_ref.dtype)


def prepare_kernel(n, gain_ref, *refs):
    pieces, lhs_ref, squares_ref = refs[:n], refs[-2], refs[-1]
    rows = jnp.concatenate([p[...].astype(jnp.float32) for p in pieces], axis=0)
    squared = (rows * rows).astype(jnp.bfloat16)
    ones = jnp.ones((8, rows.shape[1]), jnp.bfloat16)
    sums = lax.dot_general(ones, squared, (((1,), (1,)), ((), ())), preferred_element_type=jnp.float32)
    high = sums.astype(jnp.bfloat16).astype(jnp.float32)
    low = sums - high
    which = lax.broadcasted_iota(jnp.int32, sums.shape, 0)
    squares_ref[...] = jnp.where(which == 0, high, jnp.where(which == 1, low, 0.0))
    lhs_ref[...] = (rows * gain_ref[...].astype(jnp.float32)).astype(jnp.bfloat16)


def extra_rows(rows, width):
    return -(-2 * -(-rows // width) // 8) * 8


def gate_kernel(block_ref, lhs_ref, squares_ref, w_ref, *refs):
    out_ref = refs[-1]
    rows = lhs_ref.shape[0]
    width = out_ref.shape[1]
    extra = extra_rows(rows, width)
    product = jnp.dot(lhs_ref[...], w_ref[0], preferred_element_type=jnp.float32)
    squares = squares_ref[...]
    pieces = -(-rows // width)
    if rows % width:
        squares = jnp.concatenate([squares, jnp.zeros((8, width - rows % width), jnp.float32)], axis=1)
    if pieces == 1:
        below = squares
    else:
        below = jnp.concatenate(
            [squares[0:2, i * width : (i + 1) * width] for i in range(pieces)]
            + ([jnp.zeros((extra - 2 * pieces, width), jnp.float32)] if extra > 2 * pieces else []),
            axis=0,
        )
    out_ref[...] = jnp.concatenate([product, below], axis=0).astype(jnp.bfloat16)


def activate_kernel(n, rows, features, *refs):
    parts, out_ref = refs[:n], refs[-1]
    f32, bf16 = jnp.float32, jnp.bfloat16
    width = out_ref.shape[1]
    total, squares = None, None
    for part in parts:
        value = part[...].astype(f32)
        gate = value[:rows]
        extra = value[rows:]
        total = gate if total is None else total + gate
        squares = extra if squares is None else squares + extra
    pieces = -(-rows // width)
    lines = [squares[2 * i : 2 * i + 1] + squares[2 * i + 1 : 2 * i + 2] for i in range(pieces)]
    line = (lines[0] if pieces == 1 else jnp.concatenate(lines, axis=1))[:, :rows]
    inverse = lax.rsqrt(line / features + 1e-06)
    column = jnp.transpose(jnp.broadcast_to(inverse, (8, rows)))[:, 0:1]
    gate = total * column
    out_ref[...] = (gate / (1.0 + jnp.exp(-gate))).astype(bf16)


def down_kernel(steps, cap, adds, block_ref, w_ref, *refs):
    pieces, outs = refs[: len(steps)], refs[len(steps) :]
    width = pieces[0].shape[1]
    total = None
    if adds:
        total, outs = outs[0][...], outs[1:]
    for i, k in enumerate(steps):
        start = pl.multiple_of((block_ref[0] ^ k) * width, width)
        term = jnp.dot(pieces[i][...], w_ref[0, pl.ds(start, width), :], preferred_element_type=jnp.float32)
        total = term if total is None else total + term
    if cap is None:
        outs[-1][...] = total
    else:
        for i, out in enumerate(outs):
            out[...] = total[i * cap : (i + 1) * cap, :].astype(jnp.bfloat16)


def combine_kernel(n, high_ref, low_ref, *refs):
    pieces, out_ref = refs[:n], refs[n]
    rows = jnp.concatenate([p[...].astype(jnp.float32) for p in pieces], axis=0).astype(jnp.bfloat16)
    total = jnp.dot(high_ref[...], rows, preferred_element_type=jnp.float32)
    total += jnp.dot(low_ref[...], rows, preferred_element_type=jnp.float32)
    out_ref[...] = total.astype(jnp.bfloat16)


def estimate(flops, moved):
    return pl.CostEstimate(flops=int(flops), bytes_accessed=int(moved), transcendentals=0)


def local(residual, attn_partial, norm_gain, expert_ids, route_scores, w_gate, w_down):
    bf16, f32 = jnp.bfloat16, jnp.float32
    tokens, share = residual.shape
    nt, ne = lax.axis_size("tensor"), lax.axis_size("expert")
    z, me = lax.axis_index("tensor"), lax.axis_index("expert")
    top = expert_ids.shape[1]
    cap = tokens * top // ne * 5 // 4
    rows = ne * cap
    ff = w_gate.shape[2] // nt
    me_arr = jnp.full((1,), me, jnp.int32)
    z_arr = jnp.full((1,), z, jnp.int32)
    sds = jax.ShapeDtypeStruct
    near, far = [0, 1], list(range(2, ne))

    def block(k):
        return lax.dynamic_slice(attn_partial[0], (0, k * share), (tokens, share))

    if nt == 4:
        end = (z == 0) | (z == 3)
        end_arr = jnp.where(end, 1, 0).astype(jnp.int32).reshape(1)
        relayed = exchange(block(jnp.where(end, z ^ 3, z ^ 1)), "tensor", 1)
        parts = [block(z)]
        parts.append(lax.ppermute(block(z ^ 3), "tensor", [(1, 2), (2, 1)]))
        parts.append(lax.ppermute(block(z ^ 2), "tensor", [(0, 2), (3, 1)]))
        merged = pl.pallas_call(
            merge_kernel,
            out_shape=sds((tokens, share), bf16),
            in_specs=[scalar()] + [whole()] * 3,
            out_specs=whole(),
            compiler_params=params(),
            cost_estimate=estimate(2 * tokens * share, 8 * tokens * share),
            name="merge",
        )(end_arr, block(z ^ 1), block(z ^ 2), relayed)
        parts.append(lax.ppermute(merged, "tensor", [(0, 1), (1, 3), (2, 0), (3, 2)]))
        parts.append(relayed)
    else:
        end_arr = jnp.ones((1,), jnp.int32)
        parts = [exchange(block(z ^ k), "tensor", k) if k else block(z) for k in partners(nt)]

    select, high, low = pl.pallas_call(
        functools.partial(routing_kernel, ne, cap),
        out_shape=(sds((rows, tokens), bf16), sds((tokens, rows), bf16), sds((tokens, rows), bf16)),
        in_specs=[scalar(), whole(), whole(), whole()],
        out_specs=(whole(),) * 3,
        compiler_params=params(),
        cost_estimate=estimate(10**6, 2**16),
        name="routing",
    )(me_arr, expert_ids, expert_ids.T, route_scores)

    fetched = (residual, w_gate)
    residual, w_gate = pl.pallas_call(
        fetch_kernel,
        out_shape=tuple(sds(v.shape, v.dtype) for v in fetched),
        in_specs=[anywhere()] * len(fetched),
        out_specs=(whole(),) * len(fetched),
        scratch_shapes=[pltpu.SemaphoreType.DMA((len(fetched),))],
        compiler_params=params(),
        cost_estimate=estimate(10**6, sum(2 * v.size for v in fetched)),
        name="fetch",
    )(*fetched)

    kept, *near_rows = pl.pallas_call(
        functools.partial(add_kernel, len(parts), cap, near),
        out_shape=(sds((tokens, share), bf16),) + (sds((cap, share), bf16),) * len(near),
        in_specs=[scalar()] + [whole()] * (2 + len(parts)),
        out_specs=(whole(),) * (1 + len(near)),
        compiler_params=params(),
        cost_estimate=estimate(2 * rows * tokens * share, 4 * tokens * share * nt),
        name="add",
    )(end_arr, residual, select, *parts)
    arrived = {0: near_rows[0], 1: exchange(near_rows[1], "expert", 1)}
    far_rows = pl.pallas_call(
        functools.partial(pack_kernel, cap, far),
        out_shape=(sds((cap, share), bf16),) * len(far),
        in_specs=[whole()] * 2,
        out_specs=(whole(),) * len(far),
        compiler_params=params(),
        cost_estimate=estimate(2 * rows * tokens * share, 4 * tokens * share),
        name="pack",
    )(kept, select)
    for k, value in zip(far, far_rows):
        arrived[k] = exchange(value, "expert", k)

    stored = []

    def summed_gate(ks, after=None):
        count = len(ks) * cap
        lhs, squares = pl.pallas_call(
            functools.partial(prepare_kernel, len(ks)),
            out_shape=(sds((count, share), bf16), sds((8, count), f32)),
            in_specs=[whole()] * (1 + len(ks)),
            out_specs=(whole(),) * 2,
            compiler_params=params(),
            cost_estimate=estimate(16 * count * share, 4 * count * share),
            name="prepare",
        )(norm_gain[None, :], *[arrived[k] for k in ks])
        tall = count + extra_rows(count, ff)
        gates = {}
        for k in ([1, 3, 2, 0] if nt == 4 and after is not None else partners(nt)):
            earlier = [] if after is None else [after[k or 1]]
            if k == 0 and after is not None:
                written, token = pl.pallas_call(
                    store_kernel,
                    out_shape=(sds((tokens, share), bf16), sds((8, 128), f32)),
                    in_specs=[whole(), anywhere()],
                    out_specs=(whole(), whole()),
                    compiler_params=params(),
                    cost_estimate=estimate(10**6, 4 * tokens * share),
                    name="store",
                )(kept, partial_gate)
                stored.append(written)
                earlier.append(token)
            partial_gate = pl.pallas_call(
                gate_kernel,
                out_shape=sds((tall, ff), bf16),
                grid_spec=pltpu.PrefetchScalarGridSpec(
                    num_scalar_prefetch=1,
                    grid=(1,),
                    in_specs=[
                        pl.BlockSpec((count, share), lambda i, b: (0, 0)),
                        pl.BlockSpec((8, count), lambda i, b: (0, 0)),
                        pl.BlockSpec((1, share, ff), lambda i, b: (0, 0, b[0])),
                    ]
                    + [anywhere()] * len(earlier),
                    out_specs=pl.BlockSpec((tall, ff), lambda i, b: (0, 0)),
                ),
                compiler_params=params(),
                cost_estimate=estimate(2 * count * share * ff, 2 * share * ff),
                name="gate",
            )(z_arr ^ k, lhs, squares, w_gate, *earlier)
            gates[k] = exchange(partial_gate, "tensor", k) if k else partial_gate
        return gates

    def activated(ks, gates, after=()):
        count = len(ks) * cap
        return pl.pallas_call(
            functools.partial(activate_kernel, nt, count, float(share * nt)),
            out_shape=sds((count, ff), bf16),
            in_specs=[whole()] * nt + [anywhere()] * len(after),
            out_specs=whole(),
            compiler_params=params(),
            cost_estimate=estimate(20 * count * ff, 2 * count * ff * (nt + 1)),
            name="activate",
        )(*[gates[k] for k in range(nt)], *after)

    def held(value, *after):
        return pl.pallas_call(
            hold_kernel,
            out_shape=sds(value.shape, value.dtype),
            in_specs=[whole()] + [anywhere()] * len(after),
            out_specs=whole(),
            compiler_params=params(),
            cost_estimate=estimate(10**6, 4 * value.size),
            name="hold",
        )(value, *after)

    def down(ks, hidden, steps, earlier=None, final=True, after=()):
        count = len(ks) * cap
        adds = earlier is not None
        outs = pl.pallas_call(
            functools.partial(down_kernel, steps, cap if final else None, adds),
            out_shape=(sds((cap, share), bf16),) * len(ks) if final else sds((count, share), f32),
            in_specs=[scalar(), whole()] + [whole()] * (len(steps) + adds) + [anywhere()] * len(after),
            out_specs=(whole(),) * len(ks) if final else whole(),
            compiler_params=params(),
            cost_estimate=estimate(2 * count * share * ff * len(steps), 2 * share * ff * len(steps)),
            name="down",
        )(z_arr, w_down, *[hidden[k] for k in steps], *[earlier] * adds, *after)
        return dict(zip(ks, outs)) if final else outs

    near_gates = summed_gate(near)
    far_gates = summed_gate(far, near_gates)
    near_own = activated(near, near_gates)
    near_hidden = {0: near_own, 1: exchange(near_own, "tensor", 1)}
    far_own = activated(far, far_gates, (near_own,))
    far_hidden = {k: exchange(far_own, "tensor", k) if k else far_own for k in partners(nt)}
    early = [0, 3]
    far_sum = down(far, far_hidden, early, final=False, after=(near_hidden[1],))
    near_sum = down(near, near_hidden, [0, 1], final=False, after=(far_sum,))
    waiting = held(near_own, far_sum, near_sum)
    near_hidden.update({k: exchange(waiting, "tensor", k) for k in partners(nt) if k > 1})
    results = down(far, far_hidden, [k for k in partners(nt) if k not in early], far_sum)
    results.update(down(near, near_hidden, [k for k in partners(nt) if k > 1], near_sum))
    returned = {k: exchange(value, "expert", k) if k else value for k, value in results.items()}

    moe_out = pl.pallas_call(
        functools.partial(combine_kernel, ne),
        out_shape=sds((tokens, share), bf16),
        in_specs=[whole()] * (2 + ne),
        out_specs=whole(),
        compiler_params=params(),
        cost_estimate=estimate(4 * rows * tokens * share, 2 * rows * share),
        name="combine",
    )(high, low, *[returned[k] for k in range(ne)])
    return stored[0], moe_out


def solution(mesh):
    return jax.shard_map(
        local,
        mesh=mesh,
        in_specs=(
            P(("groups", "expert"), "tensor"),
            P("tensor", ("groups", "expert"), None),
            P("tensor"),
            P(("groups", "expert"), None),
            P(("groups", "expert"), None),
            P("expert", "tensor", None),
            P("expert", None, "tensor"),
        ),
        out_specs=(P(("groups", "expert"), "tensor"), P(("groups", "expert"), "tensor")),
        check_vma=False,
    )
```

```python
import functools

import jax
import jax.numpy as jnp
from jax import lax
from jax.experimental import pallas as pl
from jax.experimental.pallas import tpu as pltpu
from jax.sharding import PartitionSpec as P


def partners(n):
    return list(range(n - 1, -1, -1))


def exchange(value, axis, step):
    n = lax.axis_size(axis)
    return lax.ppermute(value, axis, [(i, i ^ step) for i in range(n)])


def params(mib=16):
    return pltpu.CompilerParams(vmem_limit_bytes=mib << 20)


def whole():
    return pl.BlockSpec(memory_space=pltpu.VMEM)


def anywhere():
    return pl.BlockSpec(memory_space=pl.ANY)


def scalar():
    return pl.BlockSpec(memory_space=pltpu.SMEM)


def routing_kernel(n, cap, me_ref, ids_ref, idst_ref, scores_ref, select_ref, high_ref, low_ref):
    me = me_ref[0]
    tokens, top = ids_ref.shape
    f32, bf16 = jnp.float32, jnp.bfloat16
    row = lax.broadcasted_iota(jnp.int32, (tokens, tokens), 0)
    col = lax.broadcasted_iota(jnp.int32, (tokens, tokens), 1)
    before_t = jnp.where(row < col, 1.0, 0.0).astype(bf16)
    before = jnp.where(col < row, 1.0, 0.0).astype(bf16)
    scores = scores_ref[...]
    weights = 2.827 * scores / jnp.sum(scores, axis=1, keepdims=True)
    slot_t = lax.broadcasted_iota(jnp.int32, (cap, tokens), 0)
    slot = lax.broadcasted_iota(jnp.int32, (tokens, cap), 1)
    selects, highs, lows = [], [], []
    for k in range(n):
        expert = me ^ k
        named_t = jnp.zeros((1, tokens), f32)
        named = jnp.zeros((tokens, 1), f32)
        weight = jnp.zeros((tokens, 1), f32)
        for j in range(top):
            hit = jnp.where(ids_ref[:, j : j + 1] == expert, 1.0, 0.0)
            named_t += jnp.where(idst_ref[j : j + 1, :] == expert, 1.0, 0.0)
            named += hit
            weight += hit * weights[:, j : j + 1]
        place_t = jnp.dot(
            jnp.broadcast_to(named_t, (8, tokens)).astype(bf16), before_t, preferred_element_type=f32
        )[0:1, :].astype(jnp.int32)
        place = jnp.dot(
            before, jnp.broadcast_to(named, (tokens, 128)).astype(bf16), preferred_element_type=f32
        )[:, 0:1].astype(jnp.int32)
        selects.append(jnp.where(place_t == slot_t, jnp.broadcast_to(named_t, slot_t.shape), 0.0))
        full = jnp.where(place == slot, jnp.broadcast_to(weight, slot.shape), 0.0)
        high = full.astype(bf16).astype(f32)
        highs.append(high)
        lows.append(full - high)
    select_ref[...] = jnp.concatenate(selects, axis=0).astype(bf16)
    high_ref[...] = jnp.concatenate(highs, axis=1).astype(bf16)
    low_ref[...] = jnp.concatenate(lows, axis=1).astype(bf16)


def fetch_kernel(*refs):
    *pairs, sems = refs
    half = len(pairs) // 2
    copies = [pltpu.make_async_copy(pairs[i], pairs[half + i], sems.at[i]) for i in range(half)]
    for copy in copies:
        copy.start()
    for copy in copies:
        copy.wait()


def merge_kernel(end_ref, own_ref, passing_ref, relayed_ref, out_ref):
    @pl.when(end_ref[0] == 1)
    def _():
        out_ref[...] = own_ref[...]

    @pl.when(end_ref[0] == 0)
    def _():
        total = passing_ref[...].astype(jnp.float32) + relayed_ref[...].astype(jnp.float32)
        out_ref[...] = total.astype(jnp.bfloat16)


def add_kernel(n_tensor, cap, ks, last_ref, residual_ref, select_ref, *refs):
    parts, kept_ref, outs = refs[:n_tensor], refs[n_tensor], refs[n_tensor + 1 :]
    total = residual_ref[...].astype(jnp.float32)
    for part in parts[:-1]:
        total += part[...].astype(jnp.float32)
    total += jnp.where(last_ref[0] == 1, parts[-1][...].astype(jnp.float32), 0.0)
    kept_ref[...] = total.astype(jnp.bfloat16)
    pack_kernel(cap, ks, kept_ref, select_ref, *outs)


def pack_kernel(cap, ks, stream_ref, select_ref, *outs):
    first, last = ks[0] * cap, (ks[-1] + 1) * cap
    packed = jnp.dot(select_ref[first:last, :], stream_ref[...], preferred_element_type=jnp.float32)
    for i, out in enumerate(outs):
        out[...] = packed[i * cap : (i + 1) * cap, :].astype(jnp.bfloat16)


def hold_kernel(value_ref, *refs):
    refs[-1][...] = value_ref[...]


def store_kernel(values_ref, after_ref, out_ref, token_ref):
    out_ref[...] = values_ref[...]
    token_ref[...] = jnp.zeros(token_ref.shape, token_ref.dtype)


def prepare_kernel(n, gain_ref, *refs):
    pieces, lhs_ref, squares_ref = refs[:n], refs[-2], refs[-1]
    rows = jnp.concatenate([p[...].astype(jnp.float32) for p in pieces], axis=0)
    squared = (rows * rows).astype(jnp.bfloat16)
    ones = jnp.ones((8, rows.shape[1]), jnp.bfloat16)
    sums = lax.dot_general(ones, squared, (((1,), (1,)), ((), ())), preferred_element_type=jnp.float32)
    high = sums.astype(jnp.bfloat16).astype(jnp.float32)
    low = sums - high
    which = lax.broadcasted_iota(jnp.int32, sums.shape, 0)
    squares_ref[...] = jnp.where(which == 0, high, jnp.where(which == 1, low, 0.0))
    lhs_ref[...] = (rows * gain_ref[...].astype(jnp.float32)).astype(jnp.bfloat16)


def extra_rows(rows, width):
    return -(-2 * -(-rows // width) // 8) * 8


def gate_kernel(block_ref, lhs_ref, squares_ref, w_ref, *refs):
    out_ref = refs[-1]
    rows = lhs_ref.shape[0]
    width = out_ref.shape[1]
    extra = extra_rows(rows, width)
    product = jnp.dot(lhs_ref[...], w_ref[0], preferred_element_type=jnp.float32)
    squares = squares_ref[...]
    pieces = -(-rows // width)
    if rows % width:
        squares = jnp.concatenate([squares, jnp.zeros((8, width - rows % width), jnp.float32)], axis=1)
    if pieces == 1:
        below = squares
    else:
        below = jnp.concatenate(
            [squares[0:2, i * width : (i + 1) * width] for i in range(pieces)]
            + ([jnp.zeros((extra - 2 * pieces, width), jnp.float32)] if extra > 2 * pieces else []),
            axis=0,
        )
    out_ref[...] = jnp.concatenate([product, below], axis=0).astype(jnp.bfloat16)


def activate_kernel(n, rows, features, *refs):
    parts, out_ref = refs[:n], refs[-1]
    f32, bf16 = jnp.float32, jnp.bfloat16
    width = out_ref.shape[1]
    total, squares = None, None
    for part in parts:
        value = part[...].astype(f32)
        gate = value[:rows]
        extra = value[rows:]
        total = gate if total is None else total + gate
        squares = extra if squares is None else squares + extra
    pieces = -(-rows // width)
    lines = [squares[2 * i : 2 * i + 1] + squares[2 * i + 1 : 2 * i + 2] for i in range(pieces)]
    line = (lines[0] if pieces == 1 else jnp.concatenate(lines, axis=1))[:, :rows]
    inverse = lax.rsqrt(line / features + 1e-06)
    column = jnp.transpose(jnp.broadcast_to(inverse, (8, rows)))[:, 0:1]
    gate = total * column
    out_ref[...] = (gate / (1.0 + jnp.exp(-gate))).astype(bf16)


def down_kernel(steps, cap, adds, block_ref, w_ref, *refs):
    pieces, outs = refs[: len(steps)], refs[len(steps) :]
    width = pieces[0].shape[1]
    total = None
    if adds:
        total, outs = outs[0][...], outs[1:]
    for i, k in enumerate(steps):
        start = pl.multiple_of((block_ref[0] ^ k) * width, width)
        term = jnp.dot(pieces[i][...], w_ref[0, pl.ds(start, width), :], preferred_element_type=jnp.float32)
        total = term if total is None else total + term
    if cap is None:
        outs[-1][...] = total
    else:
        for i, out in enumerate(outs):
            out[...] = total[i * cap : (i + 1) * cap, :].astype(jnp.bfloat16)


def combine_kernel(n, high_ref, low_ref, *refs):
    pieces, out_ref = refs[:n], refs[n]
    rows = jnp.concatenate([p[...].astype(jnp.float32) for p in pieces], axis=0).astype(jnp.bfloat16)
    total = jnp.dot(high_ref[...], rows, preferred_element_type=jnp.float32)
    total += jnp.dot(low_ref[...], rows, preferred_element_type=jnp.float32)
    out_ref[...] = total.astype(jnp.bfloat16)


def estimate(flops, moved):
    return pl.CostEstimate(flops=int(flops), bytes_accessed=int(moved), transcendentals=0)


def local(residual, attn_partial, norm_gain, expert_ids, route_scores, w_gate, w_down):
    bf16, f32 = jnp.bfloat16, jnp.float32
    tokens, share = residual.shape
    nt, ne = lax.axis_size("tensor"), lax.axis_size("expert")
    z, me = lax.axis_index("tensor"), lax.axis_index("expert")
    top = expert_ids.shape[1]
    cap = tokens * top // ne * 5 // 4
    rows = ne * cap
    ff = w_gate.shape[2] // nt
    me_arr = jnp.full((1,), me, jnp.int32)
    z_arr = jnp.full((1,), z, jnp.int32)
    sds = jax.ShapeDtypeStruct
    near, far = [0, 1], list(range(2, ne))

    def block(k):
        return lax.dynamic_slice(attn_partial[0], (0, k * share), (tokens, share))

    if nt == 4:
        end = (z == 0) | (z == 3)
        end_arr = jnp.where(end, 1, 0).astype(jnp.int32).reshape(1)
        relayed = exchange(block(jnp.where(end, z ^ 3, z ^ 1)), "tensor", 1)
        parts = [block(z)]
        parts.append(lax.ppermute(block(z ^ 3), "tensor", [(1, 2), (2, 1)]))
        parts.append(lax.ppermute(block(z ^ 2), "tensor", [(0, 2), (3, 1)]))
        merged = pl.pallas_call(
            merge_kernel,
            out_shape=sds((tokens, share), bf16),
            in_specs=[scalar()] + [whole()] * 3,
            out_specs=whole(),
            compiler_params=params(),
            cost_estimate=estimate(2 * tokens * share, 8 * tokens * share),
            name="merge",
        )(end_arr, block(z ^ 1), block(z ^ 2), relayed)
        parts.append(lax.ppermute(merged, "tensor", [(0, 1), (1, 3), (2, 0), (3, 2)]))
        parts.append(relayed)
    else:
        end_arr = jnp.ones((1,), jnp.int32)
        parts = [exchange(block(z ^ k), "tensor", k) if k else block(z) for k in partners(nt)]

    select, high, low = pl.pallas_call(
        functools.partial(routing_kernel, ne, cap),
        out_shape=(sds((rows, tokens), bf16), sds((tokens, rows), bf16), sds((tokens, rows), bf16)),
        in_specs=[scalar(), whole(), whole(), whole()],
        out_specs=(whole(),) * 3,
        compiler_params=params(),
        cost_estimate=estimate(10**6, 2**16),
        name="routing",
    )(me_arr, expert_ids, expert_ids.T, route_scores)

    fetched = (residual, w_gate)
    residual, w_gate = pl.pallas_call(
        fetch_kernel,
        out_shape=tuple(sds(v.shape, v.dtype) for v in fetched),
        in_specs=[anywhere()] * len(fetched),
        out_specs=(whole(),) * len(fetched),
        scratch_shapes=[pltpu.SemaphoreType.DMA((len(fetched),))],
        compiler_params=params(),
        cost_estimate=estimate(10**6, sum(2 * v.size for v in fetched)),
        name="fetch",
    )(*fetched)

    kept, *near_rows = pl.pallas_call(
        functools.partial(add_kernel, len(parts), cap, near),
        out_shape=(sds((tokens, share), bf16),) + (sds((cap, share), bf16),) * len(near),
        in_specs=[scalar()] + [whole()] * (2 + len(parts)),
        out_specs=(whole(),) * (1 + len(near)),
        compiler_params=params(),
        cost_estimate=estimate(2 * rows * tokens * share, 4 * tokens * share * nt),
        name="add",
    )(end_arr, residual, select, *parts)
    arrived = {0: near_rows[0], 1: exchange(near_rows[1], "expert", 1)}
    far_rows = pl.pallas_call(
        functools.partial(pack_kernel, cap, far),
        out_shape=(sds((cap, share), bf16),) * len(far),
        in_specs=[whole()] * 2,
        out_specs=(whole(),) * len(far),
        compiler_params=params(),
        cost_estimate=estimate(2 * rows * tokens * share, 4 * tokens * share),
        name="pack",
    )(kept, select)
    for k, value in zip(far, far_rows):
        arrived[k] = exchange(value, "expert", k)

    stored = []

    def summed_gate(ks, after=None):
        count = len(ks) * cap
        lhs, squares = pl.pallas_call(
            functools.partial(prepare_kernel, len(ks)),
            out_shape=(sds((count, share), bf16), sds((8, count), f32)),
            in_specs=[whole()] * (1 + len(ks)),
            out_specs=(whole(),) * 2,
            compiler_params=params(),
            cost_estimate=estimate(16 * count * share, 4 * count * share),
            name="prepare",
        )(norm_gain[None, :], *[arrived[k] for k in ks])
        tall = count + extra_rows(count, ff)
        gates = {}
        for k in ([1, 3, 2, 0] if nt == 4 and after is not None else partners(nt)):
            earlier = [] if after is None else [after[k or 1]]
            if k == 0 and after is not None:
                earlier.append(partial_gate)
            partial_gate = pl.pallas_call(
                gate_kernel,
                out_shape=sds((tall, ff), bf16),
                grid_spec=pltpu.PrefetchScalarGridSpec(
                    num_scalar_prefetch=1,
                    grid=(1,),
                    in_specs=[
                        pl.BlockSpec((count, share), lambda i, b: (0, 0)),
                        pl.BlockSpec((8, count), lambda i, b: (0, 0)),
                        pl.BlockSpec((1, share, ff), lambda i, b: (0, 0, b[0])),
                    ]
                    + [anywhere()] * len(earlier),
                    out_specs=pl.BlockSpec((tall, ff), lambda i, b: (0, 0)),
                ),
                compiler_params=params(),
                cost_estimate=estimate(2 * count * share * ff, 2 * share * ff),
                name="gate",
            )(z_arr ^ k, lhs, squares, w_gate, *earlier)
            gates[k] = exchange(partial_gate, "tensor", k) if k else partial_gate
        return gates

    def activated(ks, gates, after=()):
        count = len(ks) * cap
        return pl.pallas_call(
            functools.partial(activate_kernel, nt, count, float(share * nt)),
            out_shape=sds((count, ff), bf16),
            in_specs=[whole()] * nt + [anywhere()] * len(after),
            out_specs=whole(),
            compiler_params=params(),
            cost_estimate=estimate(20 * count * ff, 2 * count * ff * (nt + 1)),
            name="activate",
        )(*[gates[k] for k in range(nt)], *after)

    def held(value, *after):
        return pl.pallas_call(
            hold_kernel,
            out_shape=sds(value.shape, value.dtype),
            in_specs=[whole()] + [anywhere()] * len(after),
            out_specs=whole(),
            compiler_params=params(),
            cost_estimate=estimate(10**6, 4 * value.size),
            name="hold",
        )(value, *after)

    def down(ks, hidden, steps, earlier=None, final=True, after=()):
        count = len(ks) * cap
        adds = earlier is not None
        outs = pl.pallas_call(
            functools.partial(down_kernel, steps, cap if final else None, adds),
            out_shape=(sds((cap, share), bf16),) * len(ks) if final else sds((count, share), f32),
            in_specs=[scalar(), whole()] + [whole()] * (len(steps) + adds) + [anywhere()] * len(after),
            out_specs=(whole(),) * len(ks) if final else whole(),
            compiler_params=params(),
            cost_estimate=estimate(2 * count * share * ff * len(steps), 2 * share * ff * len(steps)),
            name="down",
        )(z_arr, w_down, *[hidden[k] for k in steps], *[earlier] * adds, *after)
        return dict(zip(ks, outs)) if final else outs

    near_gates = summed_gate(near)
    far_gates = summed_gate(far, near_gates)
    near_own = activated(near, near_gates)
    near_hidden = {0: near_own, 1: exchange(near_own, "tensor", 1)}
    far_own = activated(far, far_gates)
    far_hidden = {k: exchange(far_own, "tensor", k) if k else far_own for k in partners(nt)}
    early = [0, 3]
    far_sum = down(far, far_hidden, early, final=False, after=(near_hidden[1],))
    near_sum = down(near, near_hidden, [0, 1], final=False, after=(far_own,))
    stream, token = pl.pallas_call(
        store_kernel,
        out_shape=(sds((tokens, share), bf16), sds((8, 128), f32)),
        in_specs=[whole(), anywhere()],
        out_specs=(whole(), whole()),
        compiler_params=params(),
        cost_estimate=estimate(10**6, 4 * tokens * share),
        name="store",
    )(kept, far_sum)
    waiting = held(near_own, far_sum, near_sum, token)
    near_hidden.update({k: exchange(waiting, "tensor", k) for k in partners(nt) if k > 1})
    results = down(far, far_hidden, [k for k in partners(nt) if k not in early], far_sum)
    results.update(down(near, near_hidden, [k for k in partners(nt) if k > 1], near_sum))
    returned = {k: exchange(value, "expert", k) if k else value for k, value in results.items()}

    moe_out = pl.pallas_call(
        functools.partial(combine_kernel, ne),
        out_shape=sds((tokens, share), bf16),
        in_specs=[whole()] * (2 + ne),
        out_specs=whole(),
        compiler_params=params(),
        cost_estimate=estimate(4 * rows * tokens * share, 2 * rows * share),
        name="combine",
    )(high, low, *[returned[k] for k in range(ne)])
    return stream, moe_out


def solution(mesh):
    return jax.shard_map(
        local,
        mesh=mesh,
        in_specs=(
            P(("groups", "expert"), "tensor"),
            P("tensor", ("groups", "expert"), None),
            P("tensor"),
            P(("groups", "expert"), None),
            P(("groups", "expert"), None),
            P("expert", "tensor", None),
            P("expert", None, "tensor"),
        ),
        out_specs=(P(("groups", "expert"), "tensor"), P(("groups", "expert"), "tensor")),
        check_vma=False,
    )
```

```python
import functools

import jax
import jax.numpy as jnp
from jax import lax
from jax.experimental import pallas as pl
from jax.experimental.pallas import tpu as pltpu
from jax.sharding import PartitionSpec as P


SCALE = 2.0**-20


def partners(n):
    return list(range(n - 1, -1, -1))


def exchange(value, axis, step):
    n = lax.axis_size(axis)
    return lax.ppermute(value, axis, [(i, i ^ step) for i in range(n)])


def params(mib=16):
    return pltpu.CompilerParams(vmem_limit_bytes=mib << 20)


def whole():
    return pl.BlockSpec(memory_space=pltpu.VMEM)


def anywhere():
    return pl.BlockSpec(memory_space=pl.ANY)


def scalar():
    return pl.BlockSpec(memory_space=pltpu.SMEM)


def routing_kernel(n, cap, me_ref, ids_ref, idst_ref, scores_ref, select_ref, high_ref, low_ref):
    me = me_ref[0]
    tokens, top = ids_ref.shape
    f32, bf16 = jnp.float32, jnp.bfloat16
    row = lax.broadcasted_iota(jnp.int32, (tokens, tokens), 0)
    col = lax.broadcasted_iota(jnp.int32, (tokens, tokens), 1)
    before_t = jnp.where(row < col, 1.0, 0.0).astype(bf16)
    before = jnp.where(col < row, 1.0, 0.0).astype(bf16)
    scores = scores_ref[...]
    weights = 2.827 * scores / jnp.sum(scores, axis=1, keepdims=True)
    slot_t = lax.broadcasted_iota(jnp.int32, (cap, tokens), 0)
    slot = lax.broadcasted_iota(jnp.int32, (tokens, cap), 1)
    selects, highs, lows = [], [], []
    for k in range(n):
        expert = me ^ k
        named_t = jnp.zeros((1, tokens), f32)
        named = jnp.zeros((tokens, 1), f32)
        weight = jnp.zeros((tokens, 1), f32)
        for j in range(top):
            hit = jnp.where(ids_ref[:, j : j + 1] == expert, 1.0, 0.0)
            named_t += jnp.where(idst_ref[j : j + 1, :] == expert, 1.0, 0.0)
            named += hit
            weight += hit * weights[:, j : j + 1]
        place_t = jnp.dot(
            jnp.broadcast_to(named_t, (8, tokens)).astype(bf16), before_t, preferred_element_type=f32
        )[0:1, :].astype(jnp.int32)
        place = jnp.dot(
            before, jnp.broadcast_to(named, (tokens, 128)).astype(bf16), preferred_element_type=f32
        )[:, 0:1].astype(jnp.int32)
        selects.append(jnp.where(place_t == slot_t, jnp.broadcast_to(named_t, slot_t.shape), 0.0))
        full = jnp.where(place == slot, jnp.broadcast_to(weight, slot.shape), 0.0)
        high = full.astype(bf16).astype(f32)
        highs.append(high)
        lows.append(full - high)
    select_ref[...] = jnp.concatenate(selects, axis=0).astype(bf16)
    high_ref[...] = jnp.concatenate(highs, axis=1).astype(bf16)
    low_ref[...] = jnp.concatenate(lows, axis=1).astype(bf16)


def fetch_kernel(*refs):
    *pairs, sems = refs
    half = len(pairs) // 2
    copies = [pltpu.make_async_copy(pairs[i], pairs[half + i], sems.at[i]) for i in range(half)]
    for copy in copies:
        copy.start()
    for copy in copies:
        copy.wait()


def merge_kernel(end_ref, own_ref, passing_ref, relayed_ref, out_ref):
    @pl.when(end_ref[0] == 1)
    def _():
        out_ref[...] = own_ref[...]

    @pl.when(end_ref[0] == 0)
    def _():
        total = passing_ref[...].astype(jnp.float32) + relayed_ref[...].astype(jnp.float32)
        out_ref[...] = total.astype(jnp.bfloat16)


def add_kernel(n_tensor, cap, ks, last_ref, residual_ref, select_ref, *refs):
    parts, kept_ref, outs = refs[:n_tensor], refs[n_tensor], refs[n_tensor + 1 :]
    total = residual_ref[...].astype(jnp.float32)
    for part in parts[:-1]:
        total += part[...].astype(jnp.float32)
    total += jnp.where(last_ref[0] == 1, parts[-1][...].astype(jnp.float32), 0.0)
    kept_ref[...] = total.astype(jnp.bfloat16)
    pack_kernel(cap, ks, kept_ref, select_ref, *outs)


def pack_kernel(cap, ks, stream_ref, select_ref, *outs):
    first, last = ks[0] * cap, (ks[-1] + 1) * cap
    packed = jnp.dot(select_ref[first:last, :], stream_ref[...], preferred_element_type=jnp.float32)
    for i, out in enumerate(outs):
        out[...] = packed[i * cap : (i + 1) * cap, :].astype(jnp.bfloat16)


def hold_kernel(value_ref, *refs):
    refs[-1][...] = value_ref[...]


def store_kernel(values_ref, after_ref, out_ref, token_ref):
    out_ref[...] = values_ref[...]
    token_ref[...] = jnp.zeros(token_ref.shape, token_ref.dtype)


def prepare_kernel(n, gain_ref, *refs):
    pieces, lhs_ref, squares_ref = refs[:n], refs[-2], refs[-1]
    rows = jnp.concatenate([p[...].astype(jnp.float32) for p in pieces], axis=0)
    scaled = rows * SCALE
    squared = (scaled * scaled).astype(jnp.bfloat16)
    ones = jnp.ones((8, rows.shape[1]), jnp.bfloat16)
    sums = lax.dot_general(ones, squared, (((1,), (1,)), ((), ())), preferred_element_type=jnp.float32)
    high = sums.astype(jnp.bfloat16).astype(jnp.float32)
    low = jnp.where(high < jnp.inf, sums - high, 0.0)
    which = lax.broadcasted_iota(jnp.int32, sums.shape, 0)
    squares_ref[...] = jnp.where(which == 0, high, jnp.where(which == 1, low, 0.0))
    lhs_ref[...] = (rows * gain_ref[...].astype(jnp.float32)).astype(jnp.bfloat16)


def extra_rows(rows, width):
    return -(-2 * -(-rows // width) // 8) * 8


def gate_kernel(block_ref, lhs_ref, squares_ref, w_ref, *refs):
    out_ref = refs[-1]
    rows = lhs_ref.shape[0]
    width = out_ref.shape[1]
    extra = extra_rows(rows, width)
    product = jnp.dot(lhs_ref[...], w_ref[0], preferred_element_type=jnp.float32)
    squares = squares_ref[...]
    pieces = -(-rows // width)
    if rows % width:
        squares = jnp.concatenate([squares, jnp.zeros((8, width - rows % width), jnp.float32)], axis=1)
    if pieces == 1:
        below = squares
    else:
        below = jnp.concatenate(
            [squares[0:2, i * width : (i + 1) * width] for i in range(pieces)]
            + ([jnp.zeros((extra - 2 * pieces, width), jnp.float32)] if extra > 2 * pieces else []),
            axis=0,
        )
    out_ref[...] = jnp.concatenate([product, below], axis=0).astype(jnp.bfloat16)


def activate_kernel(n, rows, features, *refs):
    parts, out_ref = refs[:n], refs[-1]
    f32, bf16 = jnp.float32, jnp.bfloat16
    width = out_ref.shape[1]
    total, squares = None, None
    for part in parts:
        value = part[...].astype(f32)
        gate = value[:rows]
        extra = value[rows:]
        total = gate if total is None else total + gate
        squares = extra if squares is None else squares + extra
    pieces = -(-rows // width)
    lines = [squares[2 * i : 2 * i + 1] + squares[2 * i + 1 : 2 * i + 2] for i in range(pieces)]
    line = (lines[0] if pieces == 1 else jnp.concatenate(lines, axis=1))[:, :rows]
    inverse = lax.rsqrt(line * (1.0 / SCALE**2) / features + 1e-06)
    column = jnp.transpose(jnp.broadcast_to(inverse, (8, rows)))[:, 0:1]
    gate = jnp.where(column > 0.0, total * column, 0.0)
    out_ref[...] = (gate / (1.0 + jnp.exp(-gate))).astype(bf16)


def down_kernel(steps, cap, adds, block_ref, w_ref, *refs):
    pieces, outs = refs[: len(steps)], refs[len(steps) :]
    width = pieces[0].shape[1]
    total = None
    if adds:
        total, outs = outs[0][...], outs[1:]
    for i, k in enumerate(steps):
        start = pl.multiple_of((block_ref[0] ^ k) * width, width)
        term = jnp.dot(pieces[i][...], w_ref[0, pl.ds(start, width), :], preferred_element_type=jnp.float32)
        total = term if total is None else total + term
    if cap is None:
        outs[-1][...] = total
    else:
        for i, out in enumerate(outs):
            out[...] = total[i * cap : (i + 1) * cap, :].astype(jnp.bfloat16)


def combine_kernel(n, high_ref, low_ref, *refs):
    pieces, out_ref = refs[:n], refs[n]
    rows = jnp.concatenate([p[...].astype(jnp.float32) for p in pieces], axis=0).astype(jnp.bfloat16)
    total = jnp.dot(high_ref[...], rows, preferred_element_type=jnp.float32)
    total += jnp.dot(low_ref[...], rows, preferred_element_type=jnp.float32)
    out_ref[...] = total.astype(jnp.bfloat16)


def estimate(flops, moved):
    return pl.CostEstimate(flops=int(flops), bytes_accessed=int(moved), transcendentals=0)


def local(residual, attn_partial, norm_gain, expert_ids, route_scores, w_gate, w_down):
    bf16, f32 = jnp.bfloat16, jnp.float32
    tokens, share = residual.shape
    nt, ne = lax.axis_size("tensor"), lax.axis_size("expert")
    z, me = lax.axis_index("tensor"), lax.axis_index("expert")
    top = expert_ids.shape[1]
    cap = tokens * top // ne * 5 // 4
    rows = ne * cap
    ff = w_gate.shape[2] // nt
    me_arr = jnp.full((1,), me, jnp.int32)
    z_arr = jnp.full((1,), z, jnp.int32)
    sds = jax.ShapeDtypeStruct
    near, far = [0, 1], list(range(2, ne))

    def block(k):
        return lax.dynamic_slice(attn_partial[0], (0, k * share), (tokens, share))

    if nt == 4:
        end = (z == 0) | (z == 3)
        end_arr = jnp.where(end, 1, 0).astype(jnp.int32).reshape(1)
        relayed = exchange(block(jnp.where(end, z ^ 3, z ^ 1)), "tensor", 1)
        parts = [block(z)]
        parts.append(lax.ppermute(block(z ^ 3), "tensor", [(1, 2), (2, 1)]))
        parts.append(lax.ppermute(block(z ^ 2), "tensor", [(0, 2), (3, 1)]))
        merged = pl.pallas_call(
            merge_kernel,
            out_shape=sds((tokens, share), bf16),
            in_specs=[scalar()] + [whole()] * 3,
            out_specs=whole(),
            compiler_params=params(),
            cost_estimate=estimate(2 * tokens * share, 8 * tokens * share),
            name="merge",
        )(end_arr, block(z ^ 1), block(z ^ 2), relayed)
        parts.append(lax.ppermute(merged, "tensor", [(0, 1), (1, 3), (2, 0), (3, 2)]))
        parts.append(relayed)
    else:
        end_arr = jnp.ones((1,), jnp.int32)
        parts = [exchange(block(z ^ k), "tensor", k) if k else block(z) for k in partners(nt)]

    select, high, low = pl.pallas_call(
        functools.partial(routing_kernel, ne, cap),
        out_shape=(sds((rows, tokens), bf16), sds((tokens, rows), bf16), sds((tokens, rows), bf16)),
        in_specs=[scalar(), whole(), whole(), whole()],
        out_specs=(whole(),) * 3,
        compiler_params=params(),
        cost_estimate=estimate(10**6, 2**16),
        name="routing",
    )(me_arr, expert_ids, expert_ids.T, route_scores)

    fetched = (residual, w_gate)
    residual, w_gate = pl.pallas_call(
        fetch_kernel,
        out_shape=tuple(sds(v.shape, v.dtype) for v in fetched),
        in_specs=[anywhere()] * len(fetched),
        out_specs=(whole(),) * len(fetched),
        scratch_shapes=[pltpu.SemaphoreType.DMA((len(fetched),))],
        compiler_params=params(),
        cost_estimate=estimate(10**6, sum(2 * v.size for v in fetched)),
        name="fetch",
    )(*fetched)

    kept, *near_rows = pl.pallas_call(
        functools.partial(add_kernel, len(parts), cap, near),
        out_shape=(sds((tokens, share), bf16),) + (sds((cap, share), bf16),) * len(near),
        in_specs=[scalar()] + [whole()] * (2 + len(parts)),
        out_specs=(whole(),) * (1 + len(near)),
        compiler_params=params(),
        cost_estimate=estimate(2 * rows * tokens * share, 4 * tokens * share * nt),
        name="add",
    )(end_arr, residual, select, *parts)
    arrived = {0: near_rows[0], 1: exchange(near_rows[1], "expert", 1)}
    far_rows = pl.pallas_call(
        functools.partial(pack_kernel, cap, far),
        out_shape=(sds((cap, share), bf16),) * len(far),
        in_specs=[whole()] * 2,
        out_specs=(whole(),) * len(far),
        compiler_params=params(),
        cost_estimate=estimate(2 * rows * tokens * share, 4 * tokens * share),
        name="pack",
    )(kept, select)
    for k, value in zip(far, far_rows):
        arrived[k] = exchange(value, "expert", k)

    stored = []

    def summed_gate(ks, after=None):
        count = len(ks) * cap
        lhs, squares = pl.pallas_call(
            functools.partial(prepare_kernel, len(ks)),
            out_shape=(sds((count, share), bf16), sds((8, count), f32)),
            in_specs=[whole()] * (1 + len(ks)),
            out_specs=(whole(),) * 2,
            compiler_params=params(),
            cost_estimate=estimate(16 * count * share, 4 * count * share),
            name="prepare",
        )(norm_gain[None, :], *[arrived[k] for k in ks])
        tall = count + extra_rows(count, ff)
        gates = {}
        for k in ([1, 3, 2, 0] if nt == 4 and after is not None else partners(nt)):
            earlier = [] if after is None else [after[k or 1]]
            if k == 0 and after is not None:
                earlier.append(partial_gate)
            partial_gate = pl.pallas_call(
                gate_kernel,
                out_shape=sds((tall, ff), bf16),
                grid_spec=pltpu.PrefetchScalarGridSpec(
                    num_scalar_prefetch=1,
                    grid=(1,),
                    in_specs=[
                        pl.BlockSpec((count, share), lambda i, b: (0, 0)),
                        pl.BlockSpec((8, count), lambda i, b: (0, 0)),
                        pl.BlockSpec((1, share, ff), lambda i, b: (0, 0, b[0])),
                    ]
                    + [anywhere()] * len(earlier),
                    out_specs=pl.BlockSpec((tall, ff), lambda i, b: (0, 0)),
                ),
                compiler_params=params(),
                cost_estimate=estimate(2 * count * share * ff, 2 * share * ff),
                name="gate",
            )(z_arr ^ k, lhs, squares, w_gate, *earlier)
            gates[k] = exchange(partial_gate, "tensor", k) if k else partial_gate
        return gates

    def activated(ks, gates, after=()):
        count = len(ks) * cap
        return pl.pallas_call(
            functools.partial(activate_kernel, nt, count, float(share * nt)),
            out_shape=sds((count, ff), bf16),
            in_specs=[whole()] * nt + [anywhere()] * len(after),
            out_specs=whole(),
            compiler_params=params(),
            cost_estimate=estimate(20 * count * ff, 2 * count * ff * (nt + 1)),
            name="activate",
        )(*[gates[k] for k in range(nt)], *after)

    def held(value, *after):
        return pl.pallas_call(
            hold_kernel,
            out_shape=sds(value.shape, value.dtype),
            in_specs=[whole()] + [anywhere()] * len(after),
            out_specs=whole(),
            compiler_params=params(),
            cost_estimate=estimate(10**6, 4 * value.size),
            name="hold",
        )(value, *after)

    def down(ks, hidden, steps, earlier=None, final=True, after=()):
        count = len(ks) * cap
        adds = earlier is not None
        outs = pl.pallas_call(
            functools.partial(down_kernel, steps, cap if final else None, adds),
            out_shape=(sds((cap, share), bf16),) * len(ks) if final else sds((count, share), f32),
            in_specs=[scalar(), whole()] + [whole()] * (len(steps) + adds) + [anywhere()] * len(after),
            out_specs=(whole(),) * len(ks) if final else whole(),
            compiler_params=params(),
            cost_estimate=estimate(2 * count * share * ff * len(steps), 2 * share * ff * len(steps)),
            name="down",
        )(z_arr, w_down, *[hidden[k] for k in steps], *[earlier] * adds, *after)
        return dict(zip(ks, outs)) if final else outs

    near_gates = summed_gate(near)
    far_gates = summed_gate(far, near_gates)
    near_own = activated(near, near_gates)
    near_hidden = {0: near_own, 1: exchange(near_own, "tensor", 1)}
    far_own = activated(far, far_gates)
    far_hidden = {k: exchange(far_own, "tensor", k) if k else far_own for k in partners(nt)}
    early = [0, 3]
    far_sum = down(far, far_hidden, early, final=False, after=(near_hidden[1],))
    near_sum = down(near, near_hidden, [0, 1], final=False, after=(far_own,))
    stream, token = pl.pallas_call(
        store_kernel,
        out_shape=(sds((tokens, share), bf16), sds((8, 128), f32)),
        in_specs=[whole(), anywhere()],
        out_specs=(whole(), whole()),
        compiler_params=params(),
        cost_estimate=estimate(10**6, 4 * tokens * share),
        name="store",
    )(kept, far_sum)
    waiting = held(near_own, far_sum, near_sum, token)
    near_hidden.update({k: exchange(waiting, "tensor", k) for k in partners(nt) if k > 1})
    results = down(far, far_hidden, [k for k in partners(nt) if k not in early], far_sum)
    results.update(down(near, near_hidden, [k for k in partners(nt) if k > 1], near_sum))
    returned = {k: exchange(value, "expert", k) if k else value for k, value in results.items()}

    moe_out = pl.pallas_call(
        functools.partial(combine_kernel, ne),
        out_shape=sds((tokens, share), bf16),
        in_specs=[whole()] * (2 + ne),
        out_specs=whole(),
        compiler_params=params(),
        cost_estimate=estimate(4 * rows * tokens * share, 2 * rows * share),
        name="combine",
    )(high, low, *[returned[k] for k in range(ne)])
    return stream, moe_out


def solution(mesh):
    return jax.shard_map(
        local,
        mesh=mesh,
        in_specs=(
            P(("groups", "expert"), "tensor"),
            P("tensor", ("groups", "expert"), None),
            P("tensor"),
            P(("groups", "expert"), None),
            P(("groups", "expert"), None),
            P("expert", "tensor", None),
            P("expert", None, "tensor"),
        ),
        out_specs=(P(("groups", "expert"), "tensor"), P(("groups", "expert"), "tensor")),
        check_vma=False,
    )
```

```python
import functools

import jax
import jax.numpy as jnp
from jax import lax
from jax.experimental import pallas as pl
from jax.experimental.pallas import tpu as pltpu
from jax.sharding import PartitionSpec as P


SCALE = 2.0**-20


def partners(n):
    return list(range(n - 1, -1, -1))


def exchange(value, axis, step):
    n = lax.axis_size(axis)
    return lax.ppermute(value, axis, [(i, i ^ step) for i in range(n)])


def params(mib=16):
    return pltpu.CompilerParams(vmem_limit_bytes=mib << 20)


def whole():
    return pl.BlockSpec(memory_space=pltpu.VMEM)


def anywhere():
    return pl.BlockSpec(memory_space=pl.ANY)


def scalar():
    return pl.BlockSpec(memory_space=pltpu.SMEM)


def routing_kernel(n, cap, me_ref, ids_ref, idst_ref, scores_ref, select_ref, weigh_ref):
    me = me_ref[0]
    tokens, top = ids_ref.shape
    f32, bf16 = jnp.float32, jnp.bfloat16
    row = lax.broadcasted_iota(jnp.int32, (tokens, tokens), 0)
    col = lax.broadcasted_iota(jnp.int32, (tokens, tokens), 1)
    before_t = jnp.where(row < col, 1.0, 0.0).astype(bf16)
    before = jnp.where(col < row, 1.0, 0.0).astype(bf16)
    scores = scores_ref[...]
    weights = 2.827 * scores / jnp.sum(scores, axis=1, keepdims=True)
    slot_t = lax.broadcasted_iota(jnp.int32, (cap, tokens), 0)
    slot = lax.broadcasted_iota(jnp.int32, (tokens, cap), 1)
    selects, highs, lows = [], [], []
    for k in range(n):
        expert = me ^ k
        named_t = jnp.zeros((1, tokens), f32)
        named = jnp.zeros((tokens, 1), f32)
        weight = jnp.zeros((tokens, 1), f32)
        for j in range(top):
            hit = jnp.where(ids_ref[:, j : j + 1] == expert, 1.0, 0.0)
            named_t += jnp.where(idst_ref[j : j + 1, :] == expert, 1.0, 0.0)
            named += hit
            weight += hit * weights[:, j : j + 1]
        place_t = jnp.dot(
            jnp.broadcast_to(named_t, (8, tokens)).astype(bf16), before_t, preferred_element_type=f32
        )[0:1, :].astype(jnp.int32)
        place = jnp.dot(
            before, jnp.broadcast_to(named, (tokens, 128)).astype(bf16), preferred_element_type=f32
        )[:, 0:1].astype(jnp.int32)
        selects.append(jnp.where(place_t == slot_t, jnp.broadcast_to(named_t, slot_t.shape), 0.0))
        full = jnp.where(place == slot, jnp.broadcast_to(weight, slot.shape), 0.0)
        high = full.astype(bf16).astype(f32)
        highs.append(high)
        lows.append(full - high)
    select_ref[...] = jnp.concatenate(selects, axis=0).astype(bf16)
    weigh_ref[:tokens, :] = jnp.concatenate(highs, axis=1).astype(bf16)
    weigh_ref[tokens:, :] = jnp.concatenate(lows, axis=1).astype(bf16)


def fetch_kernel(*refs):
    *pairs, sems = refs
    half = len(pairs) // 2
    copies = [pltpu.make_async_copy(pairs[i], pairs[half + i], sems.at[i]) for i in range(half)]
    for copy in copies:
        copy.start()
    for copy in copies:
        copy.wait()


def merge_kernel(end_ref, own_ref, passing_ref, relayed_ref, out_ref):
    @pl.when(end_ref[0] == 1)
    def _():
        out_ref[...] = own_ref[...]

    @pl.when(end_ref[0] == 0)
    def _():
        total = passing_ref[...].astype(jnp.float32) + relayed_ref[...].astype(jnp.float32)
        out_ref[...] = total.astype(jnp.bfloat16)


def add_kernel(n_tensor, cap, ks, last_ref, residual_ref, select_ref, *refs):
    parts, kept_ref, outs = refs[:n_tensor], refs[n_tensor], refs[n_tensor + 1 :]
    total = residual_ref[...].astype(jnp.float32)
    for part in parts[:-1]:
        total += part[...].astype(jnp.float32)
    total += jnp.where(last_ref[0] == 1, parts[-1][...].astype(jnp.float32), 0.0)
    kept_ref[...] = total.astype(jnp.bfloat16)
    pack_kernel(cap, ks, kept_ref, select_ref, *outs)


def pack_kernel(cap, ks, stream_ref, select_ref, *outs):
    first, last = ks[0] * cap, (ks[-1] + 1) * cap
    packed = jnp.dot(select_ref[first:last, :], stream_ref[...], preferred_element_type=jnp.float32)
    for i, out in enumerate(outs):
        out[...] = packed[i * cap : (i + 1) * cap, :].astype(jnp.bfloat16)


def hold_kernel(value_ref, *refs):
    refs[-1][...] = value_ref[...]


def store_kernel(values_ref, after_ref, out_ref, token_ref):
    out_ref[...] = values_ref[...]
    token_ref[...] = jnp.zeros(token_ref.shape, token_ref.dtype)


def prepare_kernel(n, gain_ref, *refs):
    pieces, lhs_ref, squares_ref = refs[:n], refs[-2], refs[-1]
    rows = jnp.concatenate([p[...].astype(jnp.float32) for p in pieces], axis=0)
    scaled = rows * SCALE
    squared = (scaled * scaled).astype(jnp.bfloat16)
    ones = jnp.ones((8, rows.shape[1]), jnp.bfloat16)
    sums = lax.dot_general(ones, squared, (((1,), (1,)), ((), ())), preferred_element_type=jnp.float32)
    high = sums.astype(jnp.bfloat16).astype(jnp.float32)
    low = jnp.where(high < jnp.inf, sums - high, 0.0)
    which = lax.broadcasted_iota(jnp.int32, sums.shape, 0)
    squares_ref[...] = jnp.where(which == 0, high, jnp.where(which == 1, low, 0.0))
    lhs_ref[...] = (rows * gain_ref[...].astype(jnp.float32)).astype(jnp.bfloat16)


def extra_rows(rows, width):
    return -(-2 * -(-rows // width) // 8) * 8


def gate_kernel(block_ref, lhs_ref, squares_ref, w_ref, *refs):
    out_ref = refs[-1]
    rows = lhs_ref.shape[0]
    width = out_ref.shape[1]
    extra = extra_rows(rows, width)
    product = jnp.dot(lhs_ref[...], w_ref[0], preferred_element_type=jnp.float32)
    squares = squares_ref[...]
    pieces = -(-rows // width)
    if rows % width:
        squares = jnp.concatenate([squares, jnp.zeros((8, width - rows % width), jnp.float32)], axis=1)
    if pieces == 1:
        below = squares
    else:
        below = jnp.concatenate(
            [squares[0:2, i * width : (i + 1) * width] for i in range(pieces)]
            + ([jnp.zeros((extra - 2 * pieces, width), jnp.float32)] if extra > 2 * pieces else []),
            axis=0,
        )
    out_ref[...] = jnp.concatenate([product, below], axis=0).astype(jnp.bfloat16)


def activate_kernel(n, rows, features, *refs):
    parts, out_ref = refs[:n], refs[-1]
    f32, bf16 = jnp.float32, jnp.bfloat16
    width = out_ref.shape[1]
    total, squares = None, None
    for part in parts:
        value = part[...].astype(f32)
        gate = value[:rows]
        extra = value[rows:]
        total = gate if total is None else total + gate
        squares = extra if squares is None else squares + extra
    pieces = -(-rows // width)
    lines = [squares[2 * i : 2 * i + 1] + squares[2 * i + 1 : 2 * i + 2] for i in range(pieces)]
    line = (lines[0] if pieces == 1 else jnp.concatenate(lines, axis=1))[:, :rows]
    inverse = lax.rsqrt(line * (1.0 / SCALE**2) / features + 1e-06)
    column = jnp.transpose(jnp.broadcast_to(inverse, (8, rows)))[:, 0:1]
    gate = jnp.where(column > 0.0, total * column, 0.0)
    out_ref[...] = (gate / (1.0 + jnp.exp(-gate))).astype(bf16)


def down_kernel(steps, cap, adds, block_ref, w_ref, *refs):
    pieces, outs = refs[: len(steps)], refs[len(steps) :]
    width = pieces[0].shape[1]
    total = None
    if adds:
        total, outs = outs[0][...], outs[1:]
    for i, k in enumerate(steps):
        start = pl.multiple_of((block_ref[0] ^ k) * width, width)
        term = jnp.dot(pieces[i][...], w_ref[0, pl.ds(start, width), :], preferred_element_type=jnp.float32)
        total = term if total is None else total + term
    if cap is None:
        outs[-1][...] = total
    else:
        for i, out in enumerate(outs):
            out[...] = total[i * cap : (i + 1) * cap, :].astype(jnp.bfloat16)


def combine_kernel(n, n_chunks, weigh_ref, *refs):
    pieces, (out_ref, result_ref, sems) = refs[:n], refs[n:]
    tokens, share = out_ref.shape
    width = share // n_chunks
    copies = []
    for i in range(n_chunks):
        columns = pl.ds(i * width, width)
        rows = jnp.concatenate([p[:, columns].astype(jnp.float32) for p in pieces], axis=0).astype(jnp.bfloat16)
        total = jnp.dot(weigh_ref[...], rows, preferred_element_type=jnp.float32)
        result_ref[:, columns] = (total[:tokens] + total[tokens:]).astype(jnp.bfloat16)
        copies.append(pltpu.make_async_copy(result_ref.at[:, columns], out_ref.at[:, columns], sems.at[i]))
        copies[i].start()
    for copy in copies:
        copy.wait()


def estimate(flops, moved):
    return pl.CostEstimate(flops=int(flops), bytes_accessed=int(moved), transcendentals=0)


def local(residual, attn_partial, norm_gain, expert_ids, route_scores, w_gate, w_down):
    bf16, f32 = jnp.bfloat16, jnp.float32
    tokens, share = residual.shape
    nt, ne = lax.axis_size("tensor"), lax.axis_size("expert")
    z, me = lax.axis_index("tensor"), lax.axis_index("expert")
    top = expert_ids.shape[1]
    cap = tokens * top // ne * 5 // 4
    rows = ne * cap
    ff = w_gate.shape[2] // nt
    me_arr = jnp.full((1,), me, jnp.int32)
    z_arr = jnp.full((1,), z, jnp.int32)
    sds = jax.ShapeDtypeStruct
    near, far = [0, 1], list(range(2, ne))

    def block(k):
        return lax.dynamic_slice(attn_partial[0], (0, k * share), (tokens, share))

    if nt == 4:
        end = (z == 0) | (z == 3)
        end_arr = jnp.where(end, 1, 0).astype(jnp.int32).reshape(1)
        relayed = exchange(block(jnp.where(end, z ^ 3, z ^ 1)), "tensor", 1)
        parts = [block(z)]
        parts.append(lax.ppermute(block(z ^ 3), "tensor", [(1, 2), (2, 1)]))
        parts.append(lax.ppermute(block(z ^ 2), "tensor", [(0, 2), (3, 1)]))
        merged = pl.pallas_call(
            merge_kernel,
            out_shape=sds((tokens, share), bf16),
            in_specs=[scalar()] + [whole()] * 3,
            out_specs=whole(),
            compiler_params=params(),
            cost_estimate=estimate(2 * tokens * share, 8 * tokens * share),
            name="merge",
        )(end_arr, block(z ^ 1), block(z ^ 2), relayed)
        parts.append(lax.ppermute(merged, "tensor", [(0, 1), (1, 3), (2, 0), (3, 2)]))
        parts.append(relayed)
    else:
        end_arr = jnp.ones((1,), jnp.int32)
        parts = [exchange(block(z ^ k), "tensor", k) if k else block(z) for k in partners(nt)]

    select, weigh = pl.pallas_call(
        functools.partial(routing_kernel, ne, cap),
        out_shape=(sds((rows, tokens), bf16), sds((2 * tokens, rows), bf16)),
        in_specs=[scalar(), whole(), whole(), whole()],
        out_specs=(whole(),) * 2,
        compiler_params=params(),
        cost_estimate=estimate(10**6, 2**16),
        name="routing",
    )(me_arr, expert_ids, expert_ids.T, route_scores)

    fetched = (residual, w_gate)
    residual, w_gate = pl.pallas_call(
        fetch_kernel,
        out_shape=tuple(sds(v.shape, v.dtype) for v in fetched),
        in_specs=[anywhere()] * len(fetched),
        out_specs=(whole(),) * len(fetched),
        scratch_shapes=[pltpu.SemaphoreType.DMA((len(fetched),))],
        compiler_params=params(),
        cost_estimate=estimate(10**6, sum(2 * v.size for v in fetched)),
        name="fetch",
    )(*fetched)

    kept, *near_rows = pl.pallas_call(
        functools.partial(add_kernel, len(parts), cap, near + far),
        out_shape=(sds((tokens, share), bf16),) + (sds((cap, share), bf16),) * ne,
        in_specs=[scalar()] + [whole()] * (2 + len(parts)),
        out_specs=(whole(),) * (1 + ne),
        compiler_params=params(),
        cost_estimate=estimate(2 * rows * tokens * share, 4 * tokens * share * nt),
        name="add",
    )(end_arr, residual, select, *parts)
    arrived = {0: near_rows[0], 1: exchange(near_rows[1], "expert", 1)}
    far_rows = near_rows[len(near) :]
    for k, value in zip(far, far_rows):
        arrived[k] = exchange(value, "expert", k)

    stored = []

    def summed_gate(ks, after=None):
        count = len(ks) * cap
        lhs, squares = pl.pallas_call(
            functools.partial(prepare_kernel, len(ks)),
            out_shape=(sds((count, share), bf16), sds((8, count), f32)),
            in_specs=[whole()] * (1 + len(ks)),
            out_specs=(whole(),) * 2,
            compiler_params=params(),
            cost_estimate=estimate(16 * count * share, 4 * count * share),
            name="prepare",
        )(norm_gain[None, :], *[arrived[k] for k in ks])
        tall = count + extra_rows(count, ff)
        gates = {}
        for k in ([1, 3, 2, 0] if nt == 4 and after is not None else partners(nt)):
            earlier = [] if after is None else [after[k or 1]]
            if k == 0 and after is not None:
                earlier.append(partial_gate)
            partial_gate = pl.pallas_call(
                gate_kernel,
                out_shape=sds((tall, ff), bf16),
                grid_spec=pltpu.PrefetchScalarGridSpec(
                    num_scalar_prefetch=1,
                    grid=(1,),
                    in_specs=[
                        pl.BlockSpec((count, share), lambda i, b: (0, 0)),
                        pl.BlockSpec((8, count), lambda i, b: (0, 0)),
                        pl.BlockSpec((1, share, ff), lambda i, b: (0, 0, b[0])),
                    ]
                    + [anywhere()] * len(earlier),
                    out_specs=pl.BlockSpec((tall, ff), lambda i, b: (0, 0)),
                ),
                compiler_params=params(),
                cost_estimate=estimate(2 * count * share * ff, 2 * share * ff),
                name="gate",
            )(z_arr ^ k, lhs, squares, w_gate, *earlier)
            gates[k] = exchange(partial_gate, "tensor", k) if k else partial_gate
        return gates

    def activated(ks, gates, after=()):
        count = len(ks) * cap
        return pl.pallas_call(
            functools.partial(activate_kernel, nt, count, float(share * nt)),
            out_shape=sds((count, ff), bf16),
            in_specs=[whole()] * nt + [anywhere()] * len(after),
            out_specs=whole(),
            compiler_params=params(),
            cost_estimate=estimate(20 * count * ff, 2 * count * ff * (nt + 1)),
            name="activate",
        )(*[gates[k] for k in range(nt)], *after)

    def held(value, *after):
        return pl.pallas_call(
            hold_kernel,
            out_shape=sds(value.shape, value.dtype),
            in_specs=[whole()] + [anywhere()] * len(after),
            out_specs=whole(),
            compiler_params=params(),
            cost_estimate=estimate(10**6, 4 * value.size),
            name="hold",
        )(value, *after)

    def down(ks, hidden, steps, earlier=None, final=True, after=()):
        count = len(ks) * cap
        adds = earlier is not None
        outs = pl.pallas_call(
            functools.partial(down_kernel, steps, cap if final else None, adds),
            out_shape=(sds((cap, share), bf16),) * len(ks) if final else sds((count, share), f32),
            in_specs=[scalar(), whole()] + [whole()] * (len(steps) + adds) + [anywhere()] * len(after),
            out_specs=(whole(),) * len(ks) if final else whole(),
            compiler_params=params(),
            cost_estimate=estimate(2 * count * share * ff * len(steps), 2 * share * ff * len(steps)),
            name="down",
        )(z_arr, w_down, *[hidden[k] for k in steps], *[earlier] * adds, *after)
        return dict(zip(ks, outs)) if final else outs

    near_gates = summed_gate(near)
    far_gates = summed_gate(far, near_gates)
    near_own = activated(near, near_gates)
    near_hidden = {0: near_own, 1: exchange(near_own, "tensor", 1)}
    far_own = activated(far, far_gates)
    far_hidden = {k: exchange(far_own, "tensor", k) if k else far_own for k in partners(nt)}
    early = [0, 3]
    far_sum = down(far, far_hidden, early, final=False, after=(near_hidden[1],))
    near_sum = down(near, near_hidden, [0, 1], final=False, after=(far_own,))
    stream, token = pl.pallas_call(
        store_kernel,
        out_shape=(sds((tokens, share), bf16), sds((8, 128), f32)),
        in_specs=[whole(), anywhere()],
        out_specs=(whole(), whole()),
        compiler_params=params(),
        cost_estimate=estimate(10**6, 4 * tokens * share),
        name="store",
    )(kept, far_sum)
    waiting = held(near_own, far_sum, near_sum, token)
    near_hidden.update({k: exchange(waiting, "tensor", k) for k in partners(nt) if k > 1})
    results = down(far, far_hidden, [k for k in partners(nt) if k not in early], far_sum)
    results.update(down(near, near_hidden, [k for k in partners(nt) if k > 1], near_sum))
    returned = {k: exchange(value, "expert", k) if k else value for k, value in results.items()}

    n_chunks = 7 if share % (128 * 7) == 0 else 1
    moe_out = pl.pallas_call(
        functools.partial(combine_kernel, ne, n_chunks),
        out_shape=sds((tokens, share), bf16),
        in_specs=[whole()] * (1 + ne),
        out_specs=anywhere(),
        scratch_shapes=[pltpu.VMEM((tokens, share), bf16), pltpu.SemaphoreType.DMA((n_chunks,))],
        compiler_params=params(),
        cost_estimate=estimate(4 * rows * tokens * share, 2 * rows * share),
        name="combine",
    )(weigh, *[returned[k] for k in range(ne)])
    return stream, moe_out


def solution(mesh):
    return jax.shard_map(
        local,
        mesh=mesh,
        in_specs=(
            P(("groups", "expert"), "tensor"),
            P("tensor", ("groups", "expert"), None),
            P("tensor"),
            P(("groups", "expert"), None),
            P(("groups", "expert"), None),
            P("expert", "tensor", None),
            P("expert", None, "tensor"),
        ),
        out_specs=(P(("groups", "expert"), "tensor"), P(("groups", "expert"), "tensor")),
        check_vma=False,
    )
```
